512 devices in a mesh: dp: 16 (over x, y), tile: 32 (over z, core).
Axes of the slice: x: 4, y: 4, z: 16, core: 2. Of those that a mesh axis runs over, the one named last changes fastest.
Arguments:
- tiles: bfloat16 [524288, 1536], P(('dp', 'tile')), may hold values from -6 to 6
- slide_of_tile: int32 [16, 32768], P('dp', 'tile'), may hold values from 0 to 15, never falling along the last dimension, each value on 1 to 8192 neighbouring positions
- labels: int32 [16, 16], P('dp'), may hold values from 0 to 1
- attn_v: bfloat16 [1536, 512], replicated, may hold values from -0.15625 to 0.15625
- attn_u: bfloat16 [1536, 512], replicated, may hold values from -0.15625 to 0.15625
- score_w: bfloat16 [512, 8], replicated, may hold values from -200 to 200
- head_w1: bfloat16 [1536, 512], P('tile'), may hold values from -0.15625 to 0.15625
- head_w2: bfloat16 [512], replicated, may hold values from -0.25 to 0.25
Outputs:
- grad_w1: float32 [1536, 512], P('tile')
- grad_score: float32 [512, 8], replicated
- grad_w2: float32 [512], replicated
- mean_loss: float32 [], replicated
The draws below stay inside these ranges and needn't reach their ends.
Inputs may be any that keep to these rules, and one draw needn't show every extreme that they name: In each row of slide_of_tile the slide numbers never fall; every slide 0 to 15 holds 1 to 8192 tiles, and one slide of each row holds exactly 8192.
All inputs are finite; a program needn't handle non-finite values.
Results may differ from the reference program's by a relative error of at most 0.0055.
The reference program's roundings to bfloat16 on the way (of `gated` and `normed_low`) count: a program that leaves them out, or rounds other values in their place, can miss the bound.
Values may be sent and summed in bfloat16 or wider, within the bound.
A program may use at most 64 MiB of HBM per device.

```python
import math
import jax
import jax.numpy as jnp
import numpy as np
from jax import lax

E = 1536
HID = 512
HEADS = 8
SLIDES_DP = 16
GROUPS = 16
ROWS_DP = 32768
TILES = 524288


def draw_score_w(key, part):
    normal_key = jax.random.fold_in(key, 11)
    scale_key = jax.random.fold_in(key, 12)
    base_draw = jnp.clip(jax.random.normal(normal_key, (HID, HEADS), jnp.float32), -4.0, 4.0) / math.sqrt(HID)
    head_scale = jnp.exp(jax.random.uniform(scale_key, (1, HEADS), jnp.float32, 0.0, math.log(10.0)))
    return jnp.clip(base_draw * head_scale, -200.0, 200.0).astype(jnp.bfloat16)


def place_ends(drawn, stream_key, low, high):
    spot = [jax.random.randint(jax.random.fold_in(stream_key, axis), (), 0, length) for axis, length in enumerate(drawn.shape)]
    widest = drawn.shape.index(max(drawn.shape))
    neighbour = spot[:widest] + [(spot[widest] + 1) % drawn.shape[widest]] + spot[widest + 1:]
    return drawn.at[tuple(spot)].set(low).at[tuple(neighbour)].set(high)


def levels(rng, shape, cuts, least, high):
    level = 1.0
    for dim, blocks in cuts:
        heights = jax.random.uniform(jax.random.fold_in(jax.random.fold_in(rng, 6), dim), (blocks,), jnp.float32, least / len(cuts), high / len(cuts))
        level = level * jnp.repeat(jnp.exp(heights), shape[dim] // blocks).reshape((-1,) + (1,) * (len(shape) - 1 - dim))
    return level


def profile(count, total, limit, lean):
    loads = [(1 << 20) // math.isqrt(grade ** lean) + 1 for grade in range(2, count + 1)]
    spare, given = total - limit - (count - 1), [1] * (count - 1)
    while spare > 0:
        candidates = [i for i in range(count - 1) if given[i] < limit]
        pool, budget = sum([loads[i] for i in candidates]), spare
        for i in candidates:
            more = min(limit - given[i], max(1, budget * loads[i] // pool), spare)
            given[i] = given[i] + more
            spare = spare - more
    return np.array([limit] + given)


def ragged_sizes(own_key, number_of, total, most, skew):
    if number_of == 2:
        one = jax.random.randint(own_key, (), max(1, total - most), min(most, total - 1) + 1)
        return jnp.stack([one, total - one])
    lengths = jnp.asarray(profile(number_of, total, most, skew), jnp.int32)
    pairs = (number_of - 1) // 2
    giver, receiver = lengths[1:1 + 2 * pairs:2], lengths[2:2 + 2 * pairs:2]
    slack = jnp.minimum(giver - 1, most - receiver)
    shifted = jax.random.randint(jax.random.fold_in(own_key, 1), (pairs,), 0, 1 << 20) % (slack + 1)
    lengths = lengths.at[1:1 + 2 * pairs:2].set(giver - shifted).at[2:2 + 2 * pairs:2].set(receiver + shifted)
    return lengths[jax.random.permutation(jax.random.fold_in(own_key, 2), number_of)]


def scatter_about(stream_key, dims, deviation, most, pieces=(), held_as=jnp.bfloat16):
    factor_of = levels(stream_key, dims, pieces, -0.22, 0.18) if pieces else 1.0
    values = jax.random.normal(stream_key, dims, jnp.float32) * deviation * factor_of
    return jnp.minimum(jnp.maximum(values, -most), most).astype(held_as)


def setup_inputs(seed: int = 0) -> dict:
    keys = jax.random.split(jax.random.key(seed), 9)
    return {
        "tiles": scatter_about(keys[0], (TILES, E), 1.0, 6.0, ((0, 512),)),
        "slide_of_tile": jax.vmap(lambda own: jnp.searchsorted(jnp.cumsum(ragged_sizes(own, SLIDES_DP, ROWS_DP, ROWS_DP // 4, 2)), jnp.arange(ROWS_DP), side="right"))(jax.random.split(keys[1], GROUPS)).reshape((GROUPS, ROWS_DP)).astype(jnp.int32),
        "labels": place_ends(jax.random.randint(keys[2], (GROUPS, SLIDES_DP), 0, 2), jax.random.fold_in(keys[2], 1), 0, 1).astype(jnp.int32),
        "attn_v": scatter_about(keys[3], (E, HID), E ** -0.5, 0.15625),
        "attn_u": scatter_about(keys[4], (E, HID), E ** -0.5, 0.15625),
        "score_w": draw_score_w(jax.random.fold_in(keys[8], 71), 0),
        "head_w1": scatter_about(keys[6], (E, HID), E ** -0.5, 0.15625, ((0, 32),)),
        "head_w2": scatter_about(keys[7], (HID,), HID ** -0.5, 0.25),
    }


def gelu_slope(values):
    return 0.5 * (1.0 + lax.erf(values * 0.7071067811865476)) + values * jnp.exp(-0.5 * values * values) * 0.3989422804014327

def group_terms(tile_block, segment, label_row, attn_v, attn_u, score_w, head_w1, head_w2):
    row_count, feature_count = tile_block.shape
    head_count = score_w.shape[1]
    head_part = feature_count // head_count
    tanh_part = jnp.tanh(jnp.dot(tile_block, attn_v, preferred_element_type=jnp.float32))
    gate_part = jax.nn.sigmoid(jnp.dot(tile_block, attn_u, preferred_element_type=jnp.float32))
    gated = (tanh_part * gate_part).astype(jnp.bfloat16)
    scores = jnp.dot(gated, score_w, preferred_element_type=jnp.float32)
    slide_max = jax.ops.segment_max(scores, segment, num_segments=SLIDES_DP)
    expo = jnp.exp(scores - slide_max[segment])
    totals = jax.ops.segment_sum(expo, segment, num_segments=SLIDES_DP)
    split_rows = tile_block.astype(jnp.float32).reshape(row_count, head_count, head_part)
    summed = jax.ops.segment_sum(expo[:, :, None] * split_rows, segment, num_segments=SLIDES_DP)
    pooled = summed / totals[:, :, None]
    flat_pool = pooled.reshape(SLIDES_DP, feature_count)
    root_mean = jnp.sqrt(lax.optimization_barrier(jnp.mean(flat_pool * flat_pool, axis=1, keepdims=True)) + 1e-05)
    normed = flat_pool / root_mean
    normed_low = normed.astype(jnp.bfloat16)
    pre_act = jnp.dot(normed_low, head_w1, preferred_element_type=jnp.float32)
    hidden = jax.nn.gelu(pre_act, approximate=False)
    w2_float = head_w2.astype(jnp.float32)
    logits = jnp.dot(hidden, w2_float, precision=lax.Precision.HIGHEST)
    target = label_row.astype(jnp.float32)
    loss_sum = jnp.sum(jax.nn.softplus(logits) - target * logits)
    logit_grad = jax.nn.sigmoid(logits) - target
    grad_w2 = jnp.dot(logit_grad, hidden, precision=lax.Precision.HIGHEST)
    pre_grad = logit_grad[:, None] * w2_float[None, :] * gelu_slope(pre_act)
    grad_w1 = jnp.dot(normed_low.astype(jnp.float32).T, pre_grad, precision=lax.Precision.HIGHEST)
    norm_grad = jnp.dot(pre_grad, head_w1.astype(jnp.float32).T, precision=lax.Precision.HIGHEST)
    flat_grad = (norm_grad - normed * lax.optimization_barrier(jnp.mean(norm_grad * normed, axis=1, keepdims=True))) / root_mean
    pool_grad = flat_grad.reshape(SLIDES_DP, head_count, head_part)
    inner_dot = lax.optimization_barrier(jnp.sum(pooled * pool_grad, axis=2))
    projected = lax.optimization_barrier(jnp.sum(split_rows * pool_grad[segment], axis=2))
    softmax_w = expo / totals[segment]
    score_delta = softmax_w * (projected - inner_dot[segment])
    grad_score = jnp.dot(gated.astype(jnp.float32).T, score_delta, precision=lax.Precision.HIGHEST)
    return (loss_sum, grad_w1, grad_w2, grad_score)

def reference(tiles, slide_of_tile, labels, attn_v, attn_u, score_w, head_w1, head_w2):
    group_count = slide_of_tile.shape[0]
    feature_count = tiles.shape[1]
    blocks = tiles.reshape(group_count, -1, feature_count)

    def one_group(packed):
        return group_terms(packed[0], packed[1], packed[2], attn_v, attn_u, score_w, head_w1, head_w2)
    loss_sums, grad_w1s, grad_w2s, grad_scores = lax.map(one_group, (blocks, slide_of_tile, labels))
    mean_loss = jnp.sum(loss_sums) / (group_count * SLIDES_DP)
    return (lax.optimization_barrier(jnp.sum(grad_w1s, axis=0)), lax.optimization_barrier(jnp.sum(grad_scores, axis=0)), lax.optimization_barrier(jnp.sum(grad_w2s, axis=0)), mean_loss)
```

```python
import functools

import jax
import jax.numpy as jnp
from jax import lax
from jax.experimental import pallas as pl
from jax.experimental.pallas import tpu as pltpu
from jax.sharding import PartitionSpec as P

f32, bf16 = jnp.float32, jnp.bfloat16
MESH = pl.DeviceIdType.MESH
LOW = -3.0e38
BLOCK = 256
NN = (((1,), (0,)), ((), ()))
NT = (((1,), (1,)), ((), ()))
TN = (((0,), (0,)), ((), ()))


def matmul(a, b, dims=NN):
    return lax.dot_general(a, b, dims, preferred_element_type=f32)


def split(values):
    upper = values.astype(bf16)
    return upper, (values - upper.astype(f32)).astype(bf16)


def gelu_slope(values, phi):
    return phi + values * jnp.exp(-0.5 * values * values) * 0.3989422804014327


def remote(src, dst, send, recv, **where):
    return pltpu.make_async_remote_copy(
        src_ref=src, dst_ref=dst, send_sem=send, recv_sem=recv,
        device_id=where, device_id_type=MESH,
    )


def drain(ref, sem):
    pltpu.make_async_copy(ref, ref, sem).wait()


def kernel(
    tiles_hbm, seg_ref, lab_ref, v_hbm, u_hbm, sw_ref, w1_hbm, w2_ref,
    gw1_ref, gs_ref, gw2_ref, loss_ref,
    tiles, wv, wu, gated, scores, expo, w1, delta,
    swap_out, swap_in, red_out, red_in, own_half, other_half,
    wide, msg, gs_out, gs_in, gd, ga,
    load_sem, w1_sem, half_sem, red_sem, all_sem, msg_sem, gs_sem, gd_sem, ga_sem,
):
    d, t = lax.axis_index("dp"), lax.axis_index("tile")
    z, c = t // 2, t % 2
    other_t = 2 * z + 1 - c
    dx, dy = d // 4, d % 4
    rows = tiles.shape[0]

    barrier = pltpu.get_barrier_semaphore()

    def greet_tile(i, carry):
        pl.semaphore_signal(barrier, inc=1, device_id={"tile": (t + 1 + i) % 32}, device_id_type=MESH)
        return carry

    def greet_dp(i, carry):
        pl.semaphore_signal(barrier, inc=1, device_id={"dp": (d + 1 + i) % 16}, device_id_type=MESH)
        return carry

    lax.fori_loop(0, 31, greet_tile, 0)
    lax.fori_loop(0, 15, greet_dp, 0)

    loads = [
        pltpu.make_async_copy(v_hbm, wv, load_sem.at[0]),
        pltpu.make_async_copy(u_hbm, wu, load_sem.at[1]),
    ]
    for b in range(rows // BLOCK):
        part = pl.ds(b * BLOCK, BLOCK)
        loads.append(pltpu.make_async_copy(tiles_hbm.at[part], tiles.at[part], load_sem.at[2 + b]))
    own_w1 = pltpu.make_async_copy(
        w1_hbm.at[:, pl.ds(pl.multiple_of(dx * 128, 128), 128)],
        w1.at[dx, z // 4, z % 4, c], load_sem.at[7],
    )
    for load in loads:
        load.start()

    pl.semaphore_wait(barrier, 46)

    def w1_first(i):
        peer = (z + 1 + i) % 16
        return remote(
            w1_hbm.at[:, pl.ds(pl.multiple_of(dx * 128, 128), 128)],
            w1.at[dx, z // 4, z % 4, c], w1_sem.at[0], w1_sem.at[1], tile=2 * peer + c,
        )

    @pl.when(z % 4 == dy)
    def _():
        own_w1.start()

        def go(i, carry):
            w1_first(i).start()
            return carry

        lax.fori_loop(0, 15, go, 0)

    loads[0].wait()
    loads[1].wait()

    def scorer(b):
        part = pl.ds(b * BLOCK, BLOCK)
        x = tiles[part, :]
        tanh_part = jnp.tanh(matmul(x, wv[...]))
        gate_part = 0.5 + 0.5 * jnp.tanh(0.5 * matmul(x, wu[...]))
        low = (tanh_part * gate_part).astype(bf16)
        gated[part, :] = low
        scores[:, part] = matmul(sw_ref[...], low, NT)

    loads[2].wait()
    scorer(0)

    @pl.when(z % 4 == dy)
    def _():
        own_w1.wait()
        for _ in range(1):
            drain(w1.at[0, pl.ds(0, 3), 0, 0], w1_sem.at[1])

    @pl.when(z % 4 != dy)
    def _():
        drain(w1.at[0, :, 0, 0], w1_sem.at[1])

    def w1_second(i):
        part = w1.at[dx, :, dy, c]
        return remote(part, part, w1_sem.at[2], w1_sem.at[3], dp=(d + 1 + i) % 16)

    def go_second(i, carry):
        w1_second(i).start()
        return carry

    lax.fori_loop(0, 15, go_second, 0)

    for b in range(1, rows // BLOCK):
        loads[2 + b].wait()
        scorer(b)

    member = lax.broadcasted_iota(jnp.int32, (16, rows), 0) == seg_ref[...]
    lane = lax.broadcasted_iota(jnp.int32, (16, 128), 1)
    top = jnp.full((16, 128), LOW, f32)
    total = jnp.zeros((16, 128), f32)
    for k in range(8):
        score = jnp.broadcast_to(scores[k : k + 1, :], (16, rows))
        peak = jnp.max(jnp.where(member, score, LOW), axis=1, keepdims=True)
        term = jnp.where(member, jnp.exp(score - peak), 0.0)
        expo[16 * k : 16 * k + 16, :] = term
        top = jnp.where(lane == k, peak, top)
        total = jnp.where(lane == k, jnp.sum(term, axis=1, keepdims=True), total)

    blocks = []
    for q in range(4):
        upper, lower = split(expo[32 * q : 32 * q + 32, :])
        both = matmul(jnp.concatenate([upper, lower], axis=0), tiles[:, 384 * q : 384 * q + 384])
        both = both[:32] + both[32:]
        first, second = both[:16], both[16:]
        blocks += [
            first[:, :128],
            jnp.where(lane < 64, first[:, 128:256], second[:, 128:256]),
            second[:, 256:],
        ]

    def pick(a, b):
        return jnp.where(c == 0, a, b)

    def strided(j):
        return pl.ds(j, 16, stride=8)

    for j in range(6):
        swap_out[strided(j), :] = pick(blocks[6 + j], blocks[j])
    swap_out[strided(6), :] = total
    swap_out[strided(7), :] = top
    swap = remote(swap_out, swap_in, half_sem.at[0], half_sem.at[1], tile=other_t)
    swap.start()
    mine = [pick(blocks[j], blocks[6 + j]) for j in range(6)]
    swap.wait()

    low_lane = lane < 64

    def spread(table):
        heads = [pick(table[:, k : k + 1], table[:, 4 + k : 5 + k]) for k in range(4)]
        n = table.shape[0]
        heads = [jnp.broadcast_to(h, (n, 128)) for h in heads]
        low = low_lane[:n]
        return [
            heads[0], jnp.where(low, heads[0], heads[1]), heads[1],
            heads[2], jnp.where(low, heads[2], heads[3]), heads[3],
        ]

    top_other = swap_in[strided(7), :]
    pair_top = jnp.maximum(top, top_other)
    scale, scale_other = jnp.exp(top - pair_top), jnp.exp(top_other - pair_top)
    wide_own, wide_other = spread(scale), spread(scale_other)
    for j in range(6):
        red_out[strided(j), :] = mine[j] * wide_own[j] + swap_in[strided(j), :] * wide_other[j]
    red_out[strided(6), :] = total * scale + swap_in[strided(6), :] * scale_other
    red_out[strided(7), :] = pair_top

    def eight(i):
        return pl.ds(pl.multiple_of(8 * i, 8), 8)

    def reduce_copy(i):
        peer = (z + 1 + i) % 16
        return remote(red_out.at[eight(peer)], red_in.at[eight(z)], red_sem.at[0], red_sem.at[1], tile=2 * peer + c)

    def go_reduce(i, carry):
        reduce_copy(i).start()
        return carry

    lax.fori_loop(0, 15, go_reduce, 0)
    red_in[eight(z), :] = red_out[eight(z), :]

    drain(tiles_hbm.at[pl.ds(0, 240)], w1_sem.at[3])
    w1_third = remote(w1.at[:, :, :, c], w1.at[:, :, :, c], w1_sem.at[4], w1_sem.at[5], tile=other_t)
    w1_third.start()

    drain(red_in.at[pl.ds(0, 120)], red_sem.at[1])
    tops = red_in[strided(7), :]
    slide_top = jnp.max(tops, axis=0, keepdims=True)
    scale = jnp.exp(tops - slide_top)
    slide_total = jnp.sum(red_in[strided(6), :] * scale, axis=0, keepdims=True)
    wide_scale, wide_total = spread(scale), spread(slide_total)
    tile_rows = [
        jnp.sum(red_in[strided(j), :] * wide_scale[j], axis=0, keepdims=True) / wide_total[j]
        for j in range(6)
    ]
    own_half[eight(z), :] = jnp.concatenate(tile_rows + [slide_total, slide_top], axis=0)

    def gather_copy(i):
        peer = (z + 1 + i) % 16
        return remote(own_half.at[eight(z)], own_half.at[eight(z)], all_sem.at[0], all_sem.at[1], tile=2 * peer + c)

    def go_gather(i, carry):
        gather_copy(i).start()
        return carry

    lax.fori_loop(0, 15, go_gather, 0)
    drain(own_half.at[pl.ds(0, 120)], all_sem.at[1])
    relay = remote(own_half, other_half, half_sem.at[2], half_sem.at[3], tile=other_t)
    relay.start()
    w1_third.wait()
    relay.wait()

    left, right = [], []
    for j in range(6):
        a, b = own_half[strided(j), :], other_half[strided(j), :]
        left.append(pick(a, b))
        right.append(pick(b, a))
    pooled = jnp.concatenate(left + right, axis=1)
    slide_total, slide_top = own_half[strided(6), :], own_half[strided(7), :]
    width = pooled.shape[1]
    root_mean = jnp.sqrt(jnp.sum(pooled * pooled, axis=1, keepdims=True) / width + 1e-5)
    normed = pooled / root_mean
    normed_low = normed.astype(bf16)
    whole = jnp.concatenate([w1[x].reshape(width, 128) for x in range(4)], axis=1)
    pre_act = matmul(normed_low, whole)
    phi = 0.5 * (1.0 + lax.erf(pre_act * 0.7071067811865476))
    hidden = pre_act * phi
    w2_float = w2_ref[...].astype(f32)
    logits = jnp.sum(hidden * w2_float, axis=1, keepdims=True)
    square = lax.broadcasted_iota(jnp.int32, (16, 16), 0) == lax.broadcasted_iota(jnp.int32, (16, 16), 1)
    target = jnp.sum(
        jnp.where(square, jnp.broadcast_to(lab_ref[...], (16, 16)).astype(f32), 0.0), axis=1, keepdims=True
    )
    soft = jnp.exp(-jnp.abs(logits))
    loss_part = jnp.sum(jnp.maximum(logits, 0.0) + jnp.log1p(soft) - target * logits, axis=0, keepdims=True)
    logit_grad = jnp.where(logits >= 0.0, 1.0, soft) / (1.0 + soft) - target
    w2_part = jnp.sum(logit_grad * hidden, axis=0, keepdims=True)
    pre_grad = logit_grad * w2_float * gelu_slope(pre_act, phi)

    wide[:, :width] = normed_low.astype(f32)
    wide[:, width:] = jnp.zeros((16, 128), f32)
    first = 48 * t
    window = wide[:, pl.ds(pl.multiple_of(first // 128 * 128, 128), 256)].astype(bf16)
    chosen = lax.broadcasted_iota(jnp.int32, (256, 128), 0) == (
        lax.broadcasted_iota(jnp.int32, (256, 128), 1) + first % 128
    )
    normed_own = matmul(window, jnp.where(chosen, 1.0, 0.0).astype(bf16))
    sub = lax.broadcasted_iota(jnp.int32, (16, 128), 0)
    extra = jnp.zeros((16, 128), f32)
    for j in range(5):
        piece = w2_part[:, 128 * j : 128 * j + 128] if j < 4 else jnp.broadcast_to(loss_part, (1, 128))
        upper = piece.astype(bf16).astype(f32)
        extra = jnp.where(sub == j, upper, extra)
        extra = jnp.where(sub == 8 + j, piece - upper, extra)
    msg[d] = jnp.concatenate([pre_grad, normed_own, extra], axis=1).astype(bf16)

    def message(i):
        return remote(msg.at[d], msg.at[d], msg_sem.at[0], msg_sem.at[1], dp=(d + 1 + i) % 16)

    def go_message(i, carry):
        message(i).start()
        return carry

    lax.fori_loop(0, 15, go_message, 0)

    upper, lower = split(pre_grad)
    both = matmul(jnp.concatenate([upper, lower], axis=0), whole, NT)
    norm_grad = both[:16] + both[16:]
    pool_grad = (norm_grad - normed * (jnp.sum(norm_grad * normed, axis=1, keepdims=True) / width)) / root_mean

    product = pooled * pool_grad
    weight = jnp.exp(top - slide_top) / slide_total
    lane_pair = lax.broadcasted_iota(jnp.int32, (16, 384), 1)
    for q in range(4):
        grads = pool_grad[:, 384 * q : 384 * q + 384]
        terms = product[:, 384 * q : 384 * q + 384]
        pair = jnp.concatenate(
            [jnp.where(lane_pair < 192, grads, 0.0), jnp.where(lane_pair >= 192, grads, 0.0)], axis=0
        )
        upper, lower = split(pair)
        both = matmul(jnp.concatenate([upper, lower], axis=0), tiles[:, 384 * q : 384 * q + 384], NT)
        both = both[:32] + both[32:]
        for half in range(2):
            k = 2 * q + half
            side = lane_pair < 192 if half == 0 else lane_pair >= 192
            inner = jnp.sum(jnp.where(side, terms, 0.0), axis=1, keepdims=True)
            change = expo[16 * k : 16 * k + 16, :] * ((both[16 * half : 16 * half + 16] - inner) * weight[:, k : k + 1])
            delta[k : k + 1, :] = jnp.sum(change, axis=0, keepdims=True)

    upper, lower = split(delta[...])
    both = matmul(jnp.concatenate([upper, lower], axis=0), gated[...])
    score_part = both[:8] + both[8:]

    for k in range(8):
        for j in range(4):
            gs_out[4 * k + j] = score_part[k : k + 1, 128 * j : 128 * j + 128]

    def gs_reduce(i):
        peer = (t + 1 + i) % 32
        return remote(gs_out.at[peer], gs_in.at[t], gs_sem.at[0], gs_sem.at[1], tile=peer)

    def go_gs_reduce(i, carry):
        gs_reduce(i).start()
        return carry

    lax.fori_loop(0, 31, go_gs_reduce, 0)
    gs_in[t] = gs_out[t]

    drain(msg.at[pl.ds(0, 15)], msg_sem.at[1])
    grads = msg[:, :, 0:512].reshape(256, 512)
    own = msg[:, :, 512:640].reshape(256, 128)
    gw1_ref[...] = matmul(own, grads, TN)[:48]
    sums = jnp.sum(msg[:, :, 640:768].astype(f32), axis=0)
    sums = sums[:8] + sums[8:]
    gw2_ref[...] = jnp.concatenate([sums[j : j + 1] for j in range(4)], axis=1)
    loss_ref[...] = sums[4:5, 0:1] * (1.0 / 256.0)

    drain(gs_in.at[pl.ds(0, 31)], gs_sem.at[1])
    gd[d] = jnp.sum(gs_in[...], axis=0)

    def gs_dp(i):
        return remote(gd.at[d], gd.at[d], gd_sem.at[0], gd_sem.at[1], dp=(d + 1 + i) % 16)

    def go_gs_dp(i, carry):
        gs_dp(i).start()
        return carry

    lax.fori_loop(0, 15, go_gs_dp, 0)
    drain(gd.at[pl.ds(0, 15)], gd_sem.at[1])
    ga[t] = jnp.sum(gd[...], axis=0)

    def gs_gather(i):
        peer = (t + 1 + i) % 32
        return remote(ga.at[t], ga.at[t], ga_sem.at[0], ga_sem.at[1], tile=peer)

    def go_gs_gather(i, carry):
        gs_gather(i).start()
        return carry

    lax.fori_loop(0, 31, go_gs_gather, 0)
    drain(ga.at[pl.ds(0, 31)], ga_sem.at[1])
    gs_ref[...] = ga[...]

    @pl.when(z % 4 == dy)
    def _():
        def done(i, carry):
            w1_first(i).wait_send()
            return carry

        lax.fori_loop(0, 15, done, 0)

    drain(tiles_hbm.at[pl.ds(0, 240)], w1_sem.at[2])
    drain(red_in.at[pl.ds(0, 120)], red_sem.at[0])
    drain(own_half.at[pl.ds(0, 120)], all_sem.at[0])
    drain(msg.at[pl.ds(0, 15)], msg_sem.at[0])
    drain(gs_in.at[pl.ds(0, 31)], gs_sem.at[0])
    drain(gd.at[pl.ds(0, 15)], gd_sem.at[0])
    drain(ga.at[pl.ds(0, 31)], ga_sem.at[0])


def body(tiles, slide_of_tile, labels, attn_v, attn_u, score_w, head_w1, head_w2):
    rows, width = tiles.shape
    hid = attn_v.shape[1]
    vmem, hbm = pl.BlockSpec(memory_space=pltpu.VMEM), pl.BlockSpec(memory_space=pl.ANY)
    dma = pltpu.SemaphoreType.DMA
    grad_w1, grad_score, grad_w2, loss = pl.pallas_call(
        kernel,
        out_shape=(
            jax.ShapeDtypeStruct((48, hid), f32),
            jax.ShapeDtypeStruct((32, 1, 128), f32),
            jax.ShapeDtypeStruct((1, hid), f32),
            jax.ShapeDtypeStruct((1, 1), f32),
        ),
        in_specs=[hbm, vmem, vmem, hbm, hbm, vmem, hbm, vmem],
        out_specs=(vmem, vmem, vmem, vmem),
        scratch_shapes=[
            pltpu.VMEM((rows, width), bf16),
            pltpu.VMEM((width, hid), bf16),
            pltpu.VMEM((width, hid), bf16),
            pltpu.VMEM((rows, hid), bf16),
            pltpu.VMEM((8, rows), f32),
            pltpu.VMEM((128, rows), f32),
            pltpu.VMEM((4, 4, 4, 2, 48, 128), bf16),
            pltpu.VMEM((8, rows), f32),
            pltpu.VMEM((128, 128), f32),
            pltpu.VMEM((128, 128), f32),
            pltpu.VMEM((128, 128), f32),
            pltpu.VMEM((128, 128), f32),
            pltpu.VMEM((128, 128), f32),
            pltpu.VMEM((128, 128), f32),
            pltpu.VMEM((16, width + 128), f32),
            pltpu.VMEM((16, 16, 768), bf16),
            pltpu.VMEM((32, 1, 128), f32),
            pltpu.VMEM((32, 1, 128), f32),
            pltpu.VMEM((16, 1, 128), f32),
            pltpu.VMEM((32, 1, 128), f32),
            dma((8,)), dma((6,)), dma((4,)), dma((2,)), dma((2,)), dma((2,)), dma((2,)), dma((2,)), dma((2,)),
        ],
        compiler_params=pltpu.CompilerParams(
            collective_id=0, has_side_effects=True, vmem_limit_bytes=48 * 1024 * 1024
        ),
    )(tiles, slide_of_tile, labels, attn_v, attn_u, score_w.T, head_w1, head_w2.reshape(1, hid))
    return grad_w1, grad_score.reshape(8, hid).T, grad_w2.reshape(hid), loss.reshape(())


def solution(mesh):
    return jax.shard_map(
        body,
        mesh=mesh,
        in_specs=(
            P(("dp", "tile"), None),
            P("dp", "tile"),
            P("dp", None),
            P(),
            P(),
            P(),
            P("tile", None),
            P(),
        ),
        out_specs=(P("tile", None), P(), P(), P()),
        check_vma=False,
    )
```

```python
import functools

import jax
import jax.numpy as jnp
from jax import lax
from jax.experimental import pallas as pl
from jax.experimental.pallas import tpu as pltpu
from jax.sharding import PartitionSpec as P

f32, bf16 = jnp.float32, jnp.bfloat16
MESH = pl.DeviceIdType.MESH
LOW = -3.0e38
BLOCK = 256
NN = (((1,), (0,)), ((), ()))
NT = (((1,), (1,)), ((), ()))
TN = (((0,), (0,)), ((), ()))


def matmul(a, b, dims=NN):
    return lax.dot_general(a, b, dims, preferred_element_type=f32)


def split(values):
    upper = values.astype(bf16)
    return upper, (values - upper.astype(f32)).astype(bf16)


def gelu_slope(values, phi):
    return phi + values * jnp.exp(-0.5 * values * values) * 0.3989422804014327


def remote(src, dst, send, recv, **where):
    return pltpu.make_async_remote_copy(
        src_ref=src, dst_ref=dst, send_sem=send, recv_sem=recv,
        device_id=where, device_id_type=MESH,
    )


def drain(ref, sem):
    pltpu.make_async_copy(ref, ref, sem).wait()


def kernel(
    tiles_hbm, seg_hbm, lab_hbm, v_hbm, u_hbm, sw_hbm, w1_hbm, w2_hbm,
    gw1_ref, gs_ref, gw2_ref, loss_ref,
    tiles, seg, lab, wv, wu, sw, w2,
    gated, scores, expo, w1, delta,
    swap_out, swap_in, red_out, red_in, own_half, other_half,
    wide, msg, gs_out, gs_in, gz, ga,
    load_sem, w1_sem, half_sem, red_sem, all_sem, msg_sem, gs_sem, gz_sem, ga_sem,
):
    d, t = lax.axis_index("dp"), lax.axis_index("tile")
    z, c = t // 2, t % 2
    other_t = 2 * z + 1 - c
    dx, dy = d // 4, d % 4
    rows = tiles.shape[0]
    sent = []

    def finish():
        for wait in sent:
            wait()

    def loop(count, step):
        def go(i, carry):
            step(i)
            return carry

        lax.fori_loop(0, count, go, 0)

    barrier = pltpu.get_barrier_semaphore()

    place = 2 * d + c

    def plane_peer(i):
        p = (place + 1 + i) % 32
        return p, {"dp": p // 2, "tile": 2 * z + p % 2}

    def z_peer(i):
        return {"tile": 2 * ((z + 1 + i) % 16) + c}

    def greet(who):
        pl.semaphore_signal(barrier, inc=1, device_id=who, device_id_type=MESH)

    loop(31, lambda i: greet(plane_peer(i)[1]))
    loop(15, lambda i: greet(z_peer(i)))

    loads = [
        pltpu.make_async_copy(v_hbm, wv, load_sem.at[0]),
        pltpu.make_async_copy(u_hbm, wu, load_sem.at[1]),
    ]
    for b in range(rows // BLOCK):
        part = pl.ds(b * BLOCK, BLOCK)
        loads.append(pltpu.make_async_copy(tiles_hbm.at[part], tiles.at[part], load_sem.at[2 + b]))
    small = [
        pltpu.make_async_copy(sw_hbm, sw, load_sem.at[8]),
        pltpu.make_async_copy(seg_hbm, seg, load_sem.at[9]),
        pltpu.make_async_copy(lab_hbm, lab, load_sem.at[10]),
        pltpu.make_async_copy(w2_hbm, w2, load_sem.at[11]),
    ]
    own_w1 = pltpu.make_async_copy(
        w1_hbm.at[:, pl.ds(pl.multiple_of(dx * 128, 128), 128)],
        w1.at[dx, z // 4, z % 4, c], load_sem.at[7],
    )
    for load in loads + small:
        load.start()


    def w1_first(i):
        peer = (z + 1 + i) % 16
        return remote(
            w1_hbm.at[:, pl.ds(pl.multiple_of(dx * 128, 128), 128)],
            w1.at[dx, z // 4, z % 4, c], w1_sem.at[0], w1_sem.at[1], tile=2 * peer + c,
        )

    def w1_second(i):
        part = w1.at[dx, :, dy, c]
        return remote(part, part, w1_sem.at[2], w1_sem.at[3], dp=(d + 1 + i) % 16)

    w1_third = remote(w1.at[:, :, :, c], w1.at[:, :, :, c], w1_sem.at[4], w1_sem.at[5], tile=other_t)

    def w1_start():
        @pl.when(z % 4 == dy)
        def _():
            own_w1.start()
            loop(15, lambda i: w1_first(i).start())

        def wait_first():
            @pl.when(z % 4 == dy)
            def _():
                loop(15, lambda i: w1_first(i).wait_send())

        sent.append(wait_first)

    def w1_middle():
        @pl.when(z % 4 == dy)
        def _():
            own_w1.wait()
            drain(w1.at[0, pl.ds(0, 3), 0, 0], w1_sem.at[1])

        @pl.when(z % 4 != dy)
        def _():
            drain(w1.at[0, :, 0, 0], w1_sem.at[1])

        loop(15, lambda i: w1_second(i).start())
        sent.append(lambda: drain(tiles_hbm.at[pl.ds(0, 240)], w1_sem.at[2]))

    def w1_last():
        drain(tiles_hbm.at[pl.ds(0, 240)], w1_sem.at[3])
        w1_third.start()

    def w1_end():
        w1_third.wait()

    loads[0].wait()
    loads[1].wait()
    small[0].wait()

    def scorer(b):
        part = pl.ds(b * BLOCK, BLOCK)
        x = tiles[part, :]
        tanh_part = jnp.tanh(matmul(x, wv[...]))
        gate_part = 0.5 + 0.5 * jnp.tanh(0.5 * matmul(x, wu[...]))
        low = (tanh_part * gate_part).astype(bf16)
        gated[part, :] = low
        scores[:, part] = matmul(sw[...], low, NT)

    for b in range(rows // BLOCK):
        loads[2 + b].wait()
        scorer(b)
    pl.semaphore_wait(barrier, 46)
    w1_start()
    for load in small[1:]:
        load.wait()

    member = lax.broadcasted_iota(jnp.int32, (16, rows), 0) == seg[...]
    lane = lax.broadcasted_iota(jnp.int32, (16, 128), 1)
    top = jnp.full((16, 128), LOW, f32)
    total = jnp.zeros((16, 128), f32)
    for k in range(8):
        score = jnp.broadcast_to(scores[k : k + 1, :], (16, rows))
        peak = jnp.max(jnp.where(member, score, LOW), axis=1, keepdims=True)
        term = jnp.where(member, jnp.exp(score - peak), 0.0)
        expo[16 * k : 16 * k + 16, :] = term
        top = jnp.where(lane == k, peak, top)
        total = jnp.where(lane == k, jnp.sum(term, axis=1, keepdims=True), total)

    blocks = []
    for q in range(4):
        upper, lower = split(expo[32 * q : 32 * q + 32, :])
        both = matmul(jnp.concatenate([upper, lower], axis=0), tiles[:, 384 * q : 384 * q + 384])
        both = both[:32] + both[32:]
        first, second = both[:16], both[16:]
        blocks += [
            first[:, :128],
            jnp.where(lane < 64, first[:, 128:256], second[:, 128:256]),
            second[:, 256:],
        ]

    def pick(a, b):
        return jnp.where(c == 0, a, b)

    def strided(j):
        return pl.ds(j, 16, stride=8)

    for j in range(6):
        swap_out[strided(j), :] = pick(blocks[6 + j], blocks[j])
    swap_out[strided(6), :] = total
    swap_out[strided(7), :] = top
    swap = remote(swap_out, swap_in, half_sem.at[0], half_sem.at[1], tile=other_t)
    swap.start()
    mine = [pick(blocks[j], blocks[6 + j]) for j in range(6)]
    swap.wait()

    low_lane = lane < 64

    def spread(table):
        heads = [pick(table[:, k : k + 1], table[:, 4 + k : 5 + k]) for k in range(4)]
        n = table.shape[0]
        heads = [jnp.broadcast_to(h, (n, 128)) for h in heads]
        low = low_lane[:n]
        return [
            heads[0], jnp.where(low, heads[0], heads[1]), heads[1],
            heads[2], jnp.where(low, heads[2], heads[3]), heads[3],
        ]

    top_other = swap_in[strided(7), :]
    pair_top = jnp.maximum(top, top_other)
    scale, scale_other = jnp.exp(top - pair_top), jnp.exp(top_other - pair_top)
    wide_own, wide_other = spread(scale), spread(scale_other)
    for j in range(6):
        red_out[strided(j), :] = mine[j] * wide_own[j] + swap_in[strided(j), :] * wide_other[j]
    red_out[strided(6), :] = total * scale + swap_in[strided(6), :] * scale_other
    red_out[strided(7), :] = pair_top

    def eight(i):
        return pl.ds(pl.multiple_of(8 * i, 8), 8)

    def reduce_copy(i):
        peer = (z + 1 + i) % 16
        return remote(red_out.at[eight(peer)], red_in.at[eight(z)], red_sem.at[0], red_sem.at[1], tile=2 * peer + c)

    loop(15, lambda i: reduce_copy(i).start())
    sent.append(lambda: drain(red_in.at[pl.ds(0, 120)], red_sem.at[0]))
    red_in[eight(z), :] = red_out[eight(z), :]

    w1_middle()

    drain(red_in.at[pl.ds(0, 120)], red_sem.at[1])
    tops = red_in[strided(7), :]
    slide_top = jnp.max(tops, axis=0, keepdims=True)
    scale = jnp.exp(tops - slide_top)
    slide_total = jnp.sum(red_in[strided(6), :] * scale, axis=0, keepdims=True)
    wide_scale, wide_total = spread(scale), spread(slide_total)
    tile_rows = [
        jnp.sum(red_in[strided(j), :] * wide_scale[j], axis=0, keepdims=True) / wide_total[j]
        for j in range(6)
    ]
    own_half[eight(z), :] = jnp.concatenate(tile_rows + [slide_total, slide_top], axis=0)

    def gather_copy(i):
        peer = (z + 1 + i) % 16
        return remote(own_half.at[eight(z)], own_half.at[eight(z)], all_sem.at[0], all_sem.at[1], tile=2 * peer + c)

    loop(15, lambda i: gather_copy(i).start())
    sent.append(lambda: drain(own_half.at[pl.ds(0, 120)], all_sem.at[0]))
    w1_last()
    drain(own_half.at[pl.ds(0, 120)], all_sem.at[1])
    relay = remote(own_half, other_half, half_sem.at[2], half_sem.at[3], tile=other_t)
    relay.start()
    w1_end()
    relay.wait()

    left, right = [], []
    for j in range(6):
        a, b = own_half[strided(j), :], other_half[strided(j), :]
        left.append(pick(a, b))
        right.append(pick(b, a))
    pooled = jnp.concatenate(left + right, axis=1)
    slide_total, slide_top = own_half[strided(6), :], own_half[strided(7), :]
    width = pooled.shape[1]
    root_mean = jnp.sqrt(jnp.sum(pooled * pooled, axis=1, keepdims=True) / width + 1e-5)
    normed = pooled / root_mean
    normed_low = normed.astype(bf16)
    whole = jnp.concatenate([w1[x].reshape(width, 128) for x in range(4)], axis=1)
    pre_act = matmul(normed_low, whole)
    phi = 0.5 * (1.0 + lax.erf(pre_act * 0.7071067811865476))
    hidden = pre_act * phi
    w2_float = w2[...].astype(f32).reshape(1, pre_act.shape[1])
    logits = jnp.sum(hidden * w2_float, axis=1, keepdims=True)
    square = lax.broadcasted_iota(jnp.int32, (16, 16), 0) == lax.broadcasted_iota(jnp.int32, (16, 16), 1)
    target = jnp.sum(
        jnp.where(square, jnp.broadcast_to(lab[...], (16, 16)).astype(f32), 0.0), axis=1, keepdims=True
    )
    soft = jnp.exp(-jnp.abs(logits))
    loss_part = jnp.sum(jnp.maximum(logits, 0.0) + jnp.log1p(soft) - target * logits, axis=0, keepdims=True)
    logit_grad = jnp.where(logits >= 0.0, 1.0, soft) / (1.0 + soft) - target
    w2_part = jnp.sum(logit_grad * hidden, axis=0, keepdims=True)
    pre_grad = logit_grad * w2_float * gelu_slope(pre_act, phi)

    wide[:, :width] = normed_low.astype(f32)
    wide[:, width:] = jnp.zeros((16, 128), f32)
    first = 48 * t
    window = wide[:, pl.ds(pl.multiple_of(first // 128 * 128, 128), 256)].astype(bf16)
    chosen = lax.broadcasted_iota(jnp.int32, (256, 128), 0) == (
        lax.broadcasted_iota(jnp.int32, (256, 128), 1) + first % 128
    )
    normed_own = matmul(window, jnp.where(chosen, 1.0, 0.0).astype(bf16))
    sub = lax.broadcasted_iota(jnp.int32, (16, 128), 0)
    extra = jnp.zeros((16, 128), f32)
    for j in range(5):
        piece = w2_part[:, 128 * j : 128 * j + 128] if j < 4 else jnp.broadcast_to(loss_part, (1, 128))
        upper = piece.astype(bf16).astype(f32)
        extra = jnp.where(sub == j, upper, extra)
        extra = jnp.where(sub == 8 + j, piece - upper, extra)
    msg[d] = jnp.concatenate([pre_grad, normed_own, extra], axis=1).astype(bf16)

    def message(i):
        return remote(msg.at[d], msg.at[d], msg_sem.at[0], msg_sem.at[1], dp=(d + 1 + i) % 16)

    loop(15, lambda i: message(i).start())
    sent.append(lambda: drain(msg.at[pl.ds(0, 15)], msg_sem.at[0]))

    upper, lower = split(pre_grad)
    both = matmul(jnp.concatenate([upper, lower], axis=0), whole, NT)
    norm_grad = both[:16] + both[16:]
    pool_grad = (norm_grad - normed * (jnp.sum(norm_grad * normed, axis=1, keepdims=True) / width)) / root_mean

    product = pooled * pool_grad
    weight = jnp.exp(top - slide_top) / slide_total
    lane_pair = lax.broadcasted_iota(jnp.int32, (16, 384), 1)
    for q in range(4):
        grads = pool_grad[:, 384 * q : 384 * q + 384]
        terms = product[:, 384 * q : 384 * q + 384]
        pair = jnp.concatenate(
            [jnp.where(lane_pair < 192, grads, 0.0), jnp.where(lane_pair >= 192, grads, 0.0)], axis=0
        )
        upper, lower = split(pair)
        both = matmul(jnp.concatenate([upper, lower], axis=0), tiles[:, 384 * q : 384 * q + 384], NT)
        both = both[:32] + both[32:]
        for half in range(2):
            k = 2 * q + half
            side = lane_pair < 192 if half == 0 else lane_pair >= 192
            inner = jnp.sum(jnp.where(side, terms, 0.0), axis=1, keepdims=True)
            change = expo[16 * k : 16 * k + 16, :] * ((both[16 * half : 16 * half + 16] - inner) * weight[:, k : k + 1])
            delta[k : k + 1, :] = jnp.sum(change, axis=0, keepdims=True)

    upper, lower = split(delta[...])
    both = matmul(jnp.concatenate([upper, lower], axis=0), gated[...])
    score_part = both[:8] + both[8:]

    for k in range(8):
        for j in range(4):
            gs_out[4 * k + j] = score_part[k : k + 1, 128 * j : 128 * j + 128]

    def gs_plane(i):
        p, who = plane_peer(i)
        return remote(gs_out.at[p], gs_in.at[place], gs_sem.at[0], gs_sem.at[1], **who)

    loop(31, lambda i: gs_plane(i).start())
    sent.append(lambda: drain(gs_in.at[pl.ds(0, 31)], gs_sem.at[0]))
    gs_in[place] = gs_out[place]
    drain(gs_in.at[pl.ds(0, 31)], gs_sem.at[1])
    gz[z] = jnp.sum(gs_in[...], axis=0)

    def gs_z(i):
        return remote(gz.at[z], gz.at[z], gz_sem.at[0], gz_sem.at[1], **z_peer(i))

    loop(15, lambda i: gs_z(i).start())
    sent.append(lambda: drain(gz.at[pl.ds(0, 15)], gz_sem.at[0]))

    drain(msg.at[pl.ds(0, 15)], msg_sem.at[1])
    grads = msg[:, :, 0:512].reshape(256, 512)
    own = msg[:, :, 512:640].reshape(256, 128)
    gw1_ref[...] = matmul(own, grads, TN)[:48]
    sums = jnp.sum(msg[:, :, 640:768].astype(f32), axis=0)
    sums = sums[:8] + sums[8:]
    gw2_ref[...] = jnp.concatenate([sums[j : j + 1] for j in range(4)], axis=1)
    loss_ref[...] = sums[4:5, 0:1] * (1.0 / 256.0)

    drain(gz.at[pl.ds(0, 15)], gz_sem.at[1])
    ga[place] = jnp.sum(gz[...], axis=0)

    def gs_gather(i):
        return remote(ga.at[place], ga.at[place], ga_sem.at[0], ga_sem.at[1], **plane_peer(i)[1])

    loop(31, lambda i: gs_gather(i).start())
    sent.append(lambda: drain(ga.at[pl.ds(0, 31)], ga_sem.at[0]))
    drain(ga.at[pl.ds(0, 31)], ga_sem.at[1])
    for k in range(8):
        for j in range(4):
            gs_ref[k : k + 1, 128 * j : 128 * j + 128] = ga[4 * k + j]

    finish()


def body(tiles, slide_of_tile, labels, attn_v, attn_u, score_w, head_w1, head_w2):
    rows, width = tiles.shape
    hid = attn_v.shape[1]
    vmem, hbm = pl.BlockSpec(memory_space=pltpu.VMEM), pl.BlockSpec(memory_space=pltpu.HBM)
    dma = pltpu.SemaphoreType.DMA
    grad_w1, grad_score, grad_w2, loss = pl.pallas_call(
        kernel,
        out_shape=(
            jax.ShapeDtypeStruct((48, hid), f32),
            jax.ShapeDtypeStruct((8, hid), f32),
            jax.ShapeDtypeStruct((1, hid), f32),
            jax.ShapeDtypeStruct((1, 1), f32),
        ),
        in_specs=[hbm] * 8,
        out_specs=(vmem, vmem, vmem, vmem),
        scratch_shapes=[
            pltpu.VMEM((rows, width), bf16),
            pltpu.VMEM((1, rows), jnp.int32),
            pltpu.VMEM((1, 16), jnp.int32),
            pltpu.VMEM((width, hid), bf16),
            pltpu.VMEM((width, hid), bf16),
            pltpu.VMEM((8, hid), bf16),
            pltpu.VMEM((hid,), bf16),
            pltpu.VMEM((rows, hid), bf16),
            pltpu.VMEM((8, rows), f32),
            pltpu.VMEM((128, rows), f32),
            pltpu.VMEM((4, 4, 4, 2, 48, 128), bf16),
            pltpu.VMEM((8, rows), f32),
            pltpu.VMEM((128, 128), f32),
            pltpu.VMEM((128, 128), f32),
            pltpu.VMEM((128, 128), f32),
            pltpu.VMEM((128, 128), f32),
            pltpu.VMEM((128, 128), f32),
            pltpu.VMEM((128, 128), f32),
            pltpu.VMEM((16, width + 128), f32),
            pltpu.VMEM((16, 16, 768), bf16),
            pltpu.VMEM((32, 1, 128), f32),
            pltpu.VMEM((32, 1, 128), f32),
            pltpu.VMEM((16, 1, 128), f32),
            pltpu.VMEM((32, 1, 128), f32),
            dma((12,)), dma((6,)), dma((4,)), dma((2,)), dma((2,)), dma((2,)), dma((2,)), dma((2,)), dma((2,)),
        ],
        compiler_params=pltpu.CompilerParams(
            collective_id=0, has_side_effects=True, vmem_limit_bytes=60 * 1024 * 1024
        ),
    )(tiles, slide_of_tile, labels, attn_v, attn_u, score_w.T, head_w1, head_w2)
    return grad_w1, grad_score.T, grad_w2.reshape(hid), loss.reshape(())


def solution(mesh):
    return jax.shard_map(
        body,
        mesh=mesh,
        in_specs=(
            P(("dp", "tile"), None),
            P("dp", "tile"),
            P("dp", None),
            P(),
            P(),
            P(),
            P("tile", None),
            P(),
        ),
        out_specs=(P("tile", None), P(), P(), P()),
        check_vma=False,
    )
```

```python
import functools

import jax
import jax.numpy as jnp
from jax import lax
from jax.experimental import pallas as pl
from jax.experimental.pallas import tpu as pltpu
from jax.sharding import PartitionSpec as P

f32, bf16 = jnp.float32, jnp.bfloat16
MESH = pl.DeviceIdType.MESH
LOW = -3.0e38
BLOCK = 256
NN = (((1,), (0,)), ((), ()))
NT = (((1,), (1,)), ((), ()))
TN = (((0,), (0,)), ((), ()))


def matmul(a, b, dims=NN):
    return lax.dot_general(a, b, dims, preferred_element_type=f32)


def split(values):
    upper = values.astype(bf16)
    return upper, (values - upper.astype(f32)).astype(bf16)


def gelu_slope(values, phi):
    return phi + values * jnp.exp(-0.5 * values * values) * 0.3989422804014327


def remote(src, dst, send, recv, **where):
    return pltpu.make_async_remote_copy(
        src_ref=src, dst_ref=dst, send_sem=send, recv_sem=recv,
        device_id=where, device_id_type=MESH,
    )


def drain(ref, sem):
    pltpu.make_async_copy(ref, ref, sem).wait()


def kernel(
    tiles_hbm, seg_hbm, lab_hbm, v_hbm, u_hbm, sw_hbm, w1_hbm, w2_hbm,
    gw1_ref, gs_ref, gw2_ref, loss_ref,
    tiles, seg, lab, wv, wu, sw, w2,
    gated, scores, expo, w1, delta,
    swap_out, swap_in, red_out, red_in, own_half, other_half,
    wide, msg, gs_out, gs_in, gz, ga,
    load_sem, w1_sem, half_sem, red_sem, all_sem, msg_sem, gs_sem, gz_sem, ga_sem,
):
    d, t = lax.axis_index("dp"), lax.axis_index("tile")
    z, c = t // 2, t % 2
    other_t = 2 * z + 1 - c
    dx, dy = d // 4, d % 4
    rows = tiles.shape[0]
    sent = []

    def finish():
        for wait in sent:
            wait()

    def loop(count, step):
        def go(i, carry):
            step(i)
            return carry

        lax.fori_loop(0, count, go, 0)

    barrier = pltpu.get_barrier_semaphore()

    place = 2 * d + c

    def turn(i):
        return 2 + 3 * i + 3 * (i * (i - 1) // 2)

    def dp_peer(i):
        return {"dp": (dx + turn(i // 4)) % 4 * 4 + (dy + turn(i % 4)) % 4}

    def plane_peer(i):
        return {**dp_peer(i // 2), "tile": 2 * z + (c + 1 + i) % 2}

    def z_place(i):
        return (z + 8 + (1 - 2 * (i % 2)) * ((i + 1) // 2)) % 16

    def z_peer(i):
        return {"tile": 2 * z_place(i) + c}

    def greet(who):
        pl.semaphore_signal(barrier, inc=1, device_id=who, device_id_type=MESH)

    loop(31, lambda i: greet(plane_peer(i)))
    loop(15, lambda i: greet(z_peer(i)))

    loads = [
        pltpu.make_async_copy(v_hbm, wv, load_sem.at[0]),
        pltpu.make_async_copy(u_hbm, wu, load_sem.at[1]),
    ]
    for b in range(rows // BLOCK):
        part = pl.ds(b * BLOCK, BLOCK)
        loads.append(pltpu.make_async_copy(tiles_hbm.at[part], tiles.at[part], load_sem.at[2 + b]))
    small = [
        pltpu.make_async_copy(sw_hbm, sw, load_sem.at[8]),
        pltpu.make_async_copy(seg_hbm, seg, load_sem.at[9]),
        pltpu.make_async_copy(lab_hbm, lab, load_sem.at[10]),
        pltpu.make_async_copy(w2_hbm, w2, load_sem.at[11]),
    ]
    own_w1 = pltpu.make_async_copy(
        w1_hbm.at[:, pl.ds(pl.multiple_of(dx * 128, 128), 128)],
        w1.at[dx, z // 4, z % 4, c], load_sem.at[7],
    )
    for load in loads + small:
        load.start()


    def w1_first(i):
        return remote(
            w1_hbm.at[:, pl.ds(pl.multiple_of(dx * 128, 128), 128)],
            w1.at[dx, z // 4, z % 4, c], w1_sem.at[0], w1_sem.at[1], **z_peer(i),
        )

    def w1_second(i):
        part = w1.at[dx, :, dy, c]
        return remote(part, part, w1_sem.at[2], w1_sem.at[3], **dp_peer(i))

    w1_third = remote(w1.at[:, :, :, c], w1.at[:, :, :, c], w1_sem.at[4], w1_sem.at[5], tile=other_t)

    def w1_start():
        @pl.when(z % 4 == dy)
        def _():
            own_w1.start()
            loop(15, lambda i: w1_first(i).start())

        def wait_first():
            @pl.when(z % 4 == dy)
            def _():
                loop(15, lambda i: w1_first(i).wait_send())

        sent.append(wait_first)

    def w1_middle():
        @pl.when(z % 4 == dy)
        def _():
            own_w1.wait()
            drain(w1.at[0, pl.ds(0, 3), 0, 0], w1_sem.at[1])

        @pl.when(z % 4 != dy)
        def _():
            drain(w1.at[0, :, 0, 0], w1_sem.at[1])

        loop(15, lambda i: w1_second(i).start())
        sent.append(lambda: drain(tiles_hbm.at[pl.ds(0, 240)], w1_sem.at[2]))

    def w1_last():
        drain(tiles_hbm.at[pl.ds(0, 240)], w1_sem.at[3])
        w1_third.start()

    def w1_end():
        w1_third.wait()

    loads[0].wait()
    loads[1].wait()
    small[0].wait()

    def scorer(b):
        part = pl.ds(b * BLOCK, BLOCK)
        x = tiles[part, :]
        tanh_part = jnp.tanh(matmul(x, wv[...]))
        gate_part = 0.5 + 0.5 * jnp.tanh(0.5 * matmul(x, wu[...]))
        low = (tanh_part * gate_part).astype(bf16)
        gated[part, :] = low
        scores[:, part] = matmul(sw[...], low, NT)

    for b in range(rows // BLOCK):
        if b == 2:
            pl.semaphore_wait(barrier, 46)
            w1_start()
        loads[2 + b].wait()
        scorer(b)
    for load in small[1:]:
        load.wait()

    member = lax.broadcasted_iota(jnp.int32, (16, rows), 0) == seg[...]
    lane = lax.broadcasted_iota(jnp.int32, (16, 128), 1)
    top = jnp.full((16, 128), LOW, f32)
    total = jnp.zeros((16, 128), f32)
    for k in range(8):
        score = jnp.broadcast_to(scores[k : k + 1, :], (16, rows))
        peak = jnp.max(jnp.where(member, score, LOW), axis=1, keepdims=True)
        term = jnp.where(member, jnp.exp(score - peak), 0.0)
        expo[16 * k : 16 * k + 16, :] = term
        top = jnp.where(lane == k, peak, top)
        total = jnp.where(lane == k, jnp.sum(term, axis=1, keepdims=True), total)

    blocks = []
    for q in range(4):
        upper, lower = split(expo[32 * q : 32 * q + 32, :])
        both = matmul(jnp.concatenate([upper, lower], axis=0), tiles[:, 384 * q : 384 * q + 384])
        both = both[:32] + both[32:]
        first, second = both[:16], both[16:]
        blocks += [
            first[:, :128],
            jnp.where(lane < 64, first[:, 128:256], second[:, 128:256]),
            second[:, 256:],
        ]

    def pick(a, b):
        return jnp.where(c == 0, a, b)

    def strided(j):
        return pl.ds(j, 16, stride=8)

    for j in range(6):
        swap_out[strided(j), :] = pick(blocks[6 + j], blocks[j])
    swap_out[strided(6), :] = total
    swap_out[strided(7), :] = top
    swap = remote(swap_out, swap_in, half_sem.at[0], half_sem.at[1], tile=other_t)
    swap.start()
    mine = [pick(blocks[j], blocks[6 + j]) for j in range(6)]
    swap.wait()

    low_lane = lane < 64

    def spread(table):
        heads = [pick(table[:, k : k + 1], table[:, 4 + k : 5 + k]) for k in range(4)]
        n = table.shape[0]
        heads = [jnp.broadcast_to(h, (n, 128)) for h in heads]
        low = low_lane[:n]
        return [
            heads[0], jnp.where(low, heads[0], heads[1]), heads[1],
            heads[2], jnp.where(low, heads[2], heads[3]), heads[3],
        ]

    top_other = swap_in[strided(7), :]
    pair_top = jnp.maximum(top, top_other)
    scale, scale_other = jnp.exp(top - pair_top), jnp.exp(top_other - pair_top)
    wide_own, wide_other = spread(scale), spread(scale_other)
    for j in range(6):
        red_out[strided(j), :] = mine[j] * wide_own[j] + swap_in[strided(j), :] * wide_other[j]
    red_out[strided(6), :] = total * scale + swap_in[strided(6), :] * scale_other
    red_out[strided(7), :] = pair_top

    def eight(i):
        return pl.ds(pl.multiple_of(8 * i, 8), 8)

    def reduce_copy(i):
        return remote(red_out.at[eight(z_place(i))], red_in.at[eight(z)], red_sem.at[0], red_sem.at[1], **z_peer(i))

    loop(15, lambda i: reduce_copy(i).start())
    sent.append(lambda: drain(red_in.at[pl.ds(0, 120)], red_sem.at[0]))
    red_in[eight(z), :] = red_out[eight(z), :]

    w1_middle()

    drain(red_in.at[pl.ds(0, 120)], red_sem.at[1])
    tops = red_in[strided(7), :]
    slide_top = jnp.max(tops, axis=0, keepdims=True)
    scale = jnp.exp(tops - slide_top)
    slide_total = jnp.sum(red_in[strided(6), :] * scale, axis=0, keepdims=True)
    wide_scale, wide_total = spread(scale), spread(slide_total)
    tile_rows = [
        jnp.sum(red_in[strided(j), :] * wide_scale[j], axis=0, keepdims=True) / wide_total[j]
        for j in range(6)
    ]
    own_half[eight(z), :] = jnp.concatenate(tile_rows + [slide_total, slide_top], axis=0)

    def gather_copy(i):
        return remote(own_half.at[eight(z)], own_half.at[eight(z)], all_sem.at[0], all_sem.at[1], **z_peer(i))

    loop(15, lambda i: gather_copy(i).start())
    sent.append(lambda: drain(own_half.at[pl.ds(0, 120)], all_sem.at[0]))
    w1_last()
    drain(own_half.at[pl.ds(0, 120)], all_sem.at[1])
    relay = remote(own_half, other_half, half_sem.at[2], half_sem.at[3], tile=other_t)
    relay.start()
    w1_end()
    relay.wait()

    left, right = [], []
    for j in range(6):
        a, b = own_half[strided(j), :], other_half[strided(j), :]
        left.append(pick(a, b))
        right.append(pick(b, a))
    pooled = jnp.concatenate(left + right, axis=1)
    slide_total, slide_top = own_half[strided(6), :], own_half[strided(7), :]
    width = pooled.shape[1]
    root_mean = jnp.sqrt(jnp.sum(pooled * pooled, axis=1, keepdims=True) / width + 1e-5)
    normed = pooled / root_mean
    normed_low = normed.astype(bf16)
    whole = jnp.concatenate([w1[x].reshape(width, 128) for x in range(4)], axis=1)
    pre_act = matmul(normed_low, whole)
    phi = 0.5 * (1.0 + lax.erf(pre_act * 0.7071067811865476))
    hidden = pre_act * phi
    w2_float = w2[...].astype(f32).reshape(1, pre_act.shape[1])
    logits = jnp.sum(hidden * w2_float, axis=1, keepdims=True)
    square = lax.broadcasted_iota(jnp.int32, (16, 16), 0) == lax.broadcasted_iota(jnp.int32, (16, 16), 1)
    target = jnp.sum(
        jnp.where(square, jnp.broadcast_to(lab[...], (16, 16)).astype(f32), 0.0), axis=1, keepdims=True
    )
    soft = jnp.exp(-jnp.abs(logits))
    loss_part = jnp.sum(jnp.maximum(logits, 0.0) + jnp.log1p(soft) - target * logits, axis=0, keepdims=True)
    logit_grad = jnp.where(logits >= 0.0, 1.0, soft) / (1.0 + soft) - target
    w2_part = jnp.sum(logit_grad * hidden, axis=0, keepdims=True)
    pre_grad = logit_grad * w2_float * gelu_slope(pre_act, phi)

    wide[:, :width] = normed_low.astype(f32)
    wide[:, width:] = jnp.zeros((16, 128), f32)
    first = 48 * t
    window = wide[:, pl.ds(pl.multiple_of(first // 128 * 128, 128), 256)].astype(bf16)
    chosen = lax.broadcasted_iota(jnp.int32, (256, 128), 0) == (
        lax.broadcasted_iota(jnp.int32, (256, 128), 1) + first % 128
    )
    normed_own = matmul(window, jnp.where(chosen, 1.0, 0.0).astype(bf16))
    sub = lax.broadcasted_iota(jnp.int32, (16, 128), 0)
    extra = jnp.zeros((16, 128), f32)
    for j in range(5):
        piece = w2_part[:, 128 * j : 128 * j + 128] if j < 4 else jnp.broadcast_to(loss_part, (1, 128))
        upper = piece.astype(bf16).astype(f32)
        extra = jnp.where(sub == j, upper, extra)
        extra = jnp.where(sub == 8 + j, piece - upper, extra)
    msg[d] = jnp.concatenate([pre_grad, normed_own, extra], axis=1).astype(bf16)

    def message(i):
        return remote(msg.at[d], msg.at[d], msg_sem.at[0], msg_sem.at[1], **dp_peer(i))

    loop(15, lambda i: message(i).start())
    sent.append(lambda: drain(msg.at[pl.ds(0, 15)], msg_sem.at[0]))

    upper, lower = split(pre_grad)
    both = matmul(jnp.concatenate([upper, lower], axis=0), whole, NT)
    norm_grad = both[:16] + both[16:]
    pool_grad = (norm_grad - normed * (jnp.sum(norm_grad * normed, axis=1, keepdims=True) / width)) / root_mean

    product = pooled * pool_grad
    weight = jnp.exp(top - slide_top) / slide_total
    lane_pair = lax.broadcasted_iota(jnp.int32, (16, 384), 1)
    for q in range(4):
        grads = pool_grad[:, 384 * q : 384 * q + 384]
        terms = product[:, 384 * q : 384 * q + 384]
        pair = jnp.concatenate(
            [jnp.where(lane_pair < 192, grads, 0.0), jnp.where(lane_pair >= 192, grads, 0.0)], axis=0
        )
        upper, lower = split(pair)
        both = matmul(jnp.concatenate([upper, lower], axis=0), tiles[:, 384 * q : 384 * q + 384], NT)
        both = both[:32] + both[32:]
        for half in range(2):
            k = 2 * q + half
            side = lane_pair < 192 if half == 0 else lane_pair >= 192
            inner = jnp.sum(jnp.where(side, terms, 0.0), axis=1, keepdims=True)
            change = expo[16 * k : 16 * k + 16, :] * ((both[16 * half : 16 * half + 16] - inner) * weight[:, k : k + 1])
            delta[k : k + 1, :] = jnp.sum(change, axis=0, keepdims=True)

    upper, lower = split(delta[...])
    both = matmul(jnp.concatenate([upper, lower], axis=0), gated[...])
    score_part = both[:8] + both[8:]

    part, rest = score_part[:, :256], score_part[:, 256:]
    gs_out[...] = pick(rest, part)
    gs_swap = remote(gs_out, gs_in, gs_sem.at[0], gs_sem.at[1], tile=other_t)
    gs_swap.start()
    part = pick(part, rest)
    gs_swap.wait()
    part = part + gs_in[...]

    gz[z] = jnp.concatenate([part[:, :128], part[:, 128:]], axis=0).astype(bf16)

    def gs_z(i):
        return remote(gz.at[z], gz.at[z], gz_sem.at[0], gz_sem.at[1], **z_peer(i))

    loop(15, lambda i: gs_z(i).start())
    sent.append(lambda: drain(gz.at[pl.ds(0, 15)], gz_sem.at[0]))

    drain(msg.at[pl.ds(0, 15)], msg_sem.at[1])
    grads = msg[:, :, 0:512].reshape(256, 512)
    own = msg[:, :, 512:640].reshape(256, 128)
    gw1_ref[...] = matmul(own, grads, TN)[:48]
    sums = jnp.sum(msg[:, :, 640:768].astype(f32), axis=0)
    sums = sums[:8] + sums[8:]
    gw2_ref[...] = jnp.concatenate([sums[j : j + 1] for j in range(4)], axis=1)
    loss_ref[...] = sums[4:5, 0:1] * (1.0 / 256.0)

    drain(gz.at[pl.ds(0, 15)], gz_sem.at[1])

    ga[place] = jnp.sum(gz[...].astype(f32), axis=0).astype(bf16)

    def gs_plane(i):
        return remote(ga.at[place], ga.at[place], ga_sem.at[0], ga_sem.at[1], **plane_peer(i))

    loop(31, lambda i: gs_plane(i).start())
    sent.append(lambda: drain(ga.at[pl.ds(0, 31)], ga_sem.at[0]))
    drain(ga.at[pl.ds(0, 31)], ga_sem.at[1])
    parts = ga[...].astype(f32).reshape(16, 2, 16, 128)
    for half in range(2):
        sums = jnp.sum(parts[:, half], axis=0)
        gs_ref[:, 256 * half : 256 * half + 128] = sums[:8]
        gs_ref[:, 256 * half + 128 : 256 * half + 256] = sums[8:]

    finish()


def publish(*refs):
    sems = refs[8]
    copies = [pltpu.make_async_copy(refs[i], refs[4 + i], sems.at[i]) for i in range(4)]
    for copy in copies:
        copy.start()
    for copy in copies:
        copy.wait()


def body(tiles, slide_of_tile, labels, attn_v, attn_u, score_w, head_w1, head_w2):
    rows, width = tiles.shape
    hid = attn_v.shape[1]
    vmem, hbm = pl.BlockSpec(memory_space=pltpu.VMEM), pl.BlockSpec(memory_space=pltpu.HBM)
    dma = pltpu.SemaphoreType.DMA
    shapes = tuple(jax.ShapeDtypeStruct(shape, f32) for shape in ((48, hid), (8, hid), (1, hid), (1, 1)))
    results = pl.pallas_call(
        kernel,
        out_shape=shapes,
        in_specs=[hbm] * 8,
        out_specs=(vmem, vmem, vmem, vmem),
        scratch_shapes=[
            pltpu.VMEM((rows, width), bf16),
            pltpu.VMEM((1, rows), jnp.int32),
            pltpu.VMEM((1, 16), jnp.int32),
            pltpu.VMEM((width, hid), bf16),
            pltpu.VMEM((width, hid), bf16),
            pltpu.VMEM((8, hid), bf16),
            pltpu.VMEM((hid,), bf16),
            pltpu.VMEM((rows, hid), bf16),
            pltpu.VMEM((8, rows), f32),
            pltpu.VMEM((128, rows), f32),
            pltpu.VMEM((4, 4, 4, 2, 48, 128), bf16),
            pltpu.VMEM((8, rows), f32),
            pltpu.VMEM((128, 128), f32),
            pltpu.VMEM((128, 128), f32),
            pltpu.VMEM((128, 128), f32),
            pltpu.VMEM((128, 128), f32),
            pltpu.VMEM((128, 128), f32),
            pltpu.VMEM((128, 128), f32),
            pltpu.VMEM((16, width + 128), f32),
            pltpu.VMEM((16, 16, 768), bf16),
            pltpu.VMEM((8, 256), f32),
            pltpu.VMEM((8, 256), f32),
            pltpu.VMEM((16, 16, 128), bf16),
            pltpu.VMEM((32, 16, 128), bf16),
            dma((12,)), dma((6,)), dma((4,)), dma((2,)), dma((2,)), dma((2,)), dma((2,)), dma((2,)), dma((2,)),
        ],
        compiler_params=pltpu.CompilerParams(
            collective_id=0, has_side_effects=True, vmem_limit_bytes=60 * 1024 * 1024
        ),
    )(tiles, slide_of_tile, labels, attn_v, attn_u, score_w.T, head_w1, head_w2)
    grad_w1, grad_score, grad_w2, loss = pl.pallas_call(
        publish, out_shape=shapes, in_specs=[hbm] * 4, out_specs=(hbm,) * 4, scratch_shapes=[dma((4,))]
    )(*results)
    return grad_w1, grad_score.T, grad_w2.reshape(hid), loss.reshape(())


def solution(mesh):
    return jax.shard_map(
        body,
        mesh=mesh,
        in_specs=(
            P(("dp", "tile"), None),
            P("dp", "tile"),
            P("dp", None),
            P(),
            P(),
            P(),
            P("tile", None),
            P(),
        ),
        out_specs=(P("tile", None), P(), P(), P()),
        check_vma=False,
    )
```

```python
import functools

import jax
import jax.numpy as jnp
from jax import lax
from jax.experimental import pallas as pl
from jax.experimental.pallas import tpu as pltpu
from jax.sharding import PartitionSpec as P

f32, bf16 = jnp.float32, jnp.bfloat16
MESH = pl.DeviceIdType.MESH
LOW = -3.0e38
BLOCK = 256
NN = (((1,), (0,)), ((), ()))
NT = (((1,), (1,)), ((), ()))
TN = (((0,), (0,)), ((), ()))


def matmul(a, b, dims=NN):
    return lax.dot_general(a, b, dims, preferred_element_type=f32)


def split(values):
    upper = values.astype(bf16)
    return upper, (values - upper.astype(f32)).astype(bf16)


def gelu_slope(values, phi):
    return phi + values * jnp.exp(-0.5 * values * values) * 0.3989422804014327


def remote(src, dst, send, recv, **where):
    return pltpu.make_async_remote_copy(
        src_ref=src, dst_ref=dst, send_sem=send, recv_sem=recv,
        device_id=where, device_id_type=MESH,
    )


def drain(ref, sem):
    pltpu.make_async_copy(ref, ref, sem).wait()


def kernel(
    tiles_hbm, seg_hbm, lab_hbm, v_hbm, u_hbm, sw_hbm, w1_hbm, w2_hbm,
    gw1_ref, gs_ref, gw2_ref, loss_ref,
    tiles, seg, lab, wv, wu, sw, w2,
    gated, scores, expo, w1, delta,
    swap_out, swap_in, red_out, red_in, own_half, other_half,
    wide, msg, gs_out, gs_in, gz, ga,
    load_sem, w1_sem, half_sem, red_sem, all_sem, msg_sem, gs_sem, gz_sem, ga_sem,
):
    d, t = lax.axis_index("dp"), lax.axis_index("tile")
    z, c = t // 2, t % 2
    other_t = 2 * z + 1 - c
    dx, dy = d // 4, d % 4
    rows = tiles.shape[0]
    sent = []

    def finish():
        for wait in sent:
            wait()

    def loop(count, step):
        def go(i, carry):
            step(i)
            return carry

        lax.fori_loop(0, count, go, 0)

    barrier = pltpu.get_barrier_semaphore()

    place = 2 * d + c

    def turn(i):
        return 2 + 3 * i + 3 * (i * (i - 1) // 2)

    def dp_peer(i):
        return {"dp": (dx + turn(i // 4)) % 4 * 4 + (dy + turn(i % 4)) % 4}

    def plane_peer(i):
        return {**dp_peer(i // 2), "tile": 2 * z + (c + 1 + i) % 2}

    def z_place(i):
        return (z + 8 + (1 - 2 * (i % 2)) * ((i + 1) // 2)) % 16

    def z_peer(i):
        return {"tile": 2 * z_place(i) + c}

    loads = [
        pltpu.make_async_copy(v_hbm, wv, load_sem.at[0]),
        pltpu.make_async_copy(u_hbm, wu, load_sem.at[1]),
    ]
    for b in range(rows // BLOCK):
        part = pl.ds(b * BLOCK, BLOCK)
        loads.append(pltpu.make_async_copy(tiles_hbm.at[part], tiles.at[part], load_sem.at[2 + b]))
    small = [
        pltpu.make_async_copy(sw_hbm, sw, load_sem.at[8]),
        pltpu.make_async_copy(seg_hbm, seg, load_sem.at[9]),
        pltpu.make_async_copy(lab_hbm, lab, load_sem.at[10]),
        pltpu.make_async_copy(w2_hbm, w2, load_sem.at[11]),
    ]
    own_w1 = pltpu.make_async_copy(
        w1_hbm.at[:, pl.ds(pl.multiple_of(dx * 128, 128), 128)],
        w1.at[dx, z // 4, z % 4, c], load_sem.at[7],
    )
    for load in [loads[2], *loads[:2], small[0], *loads[3:], *small[1:]]:
        load.start()

    def greet(who):
        pl.semaphore_signal(barrier, inc=1, device_id=who, device_id_type=MESH)

    loop(31, lambda i: greet(plane_peer(i)))
    loop(15, lambda i: greet(z_peer(i)))


    def w1_first(i):
        return remote(
            w1_hbm.at[:, pl.ds(pl.multiple_of(dx * 128, 128), 128)],
            w1.at[dx, z // 4, z % 4, c], w1_sem.at[0], w1_sem.at[1], **z_peer(i),
        )

    def w1_second(i):
        part = w1.at[dx, :, dy, c]
        return remote(part, part, w1_sem.at[2], w1_sem.at[3], **dp_peer(i))

    w1_third = remote(w1.at[:, :, :, c], w1.at[:, :, :, c], w1_sem.at[4], w1_sem.at[5], tile=other_t)

    def w1_start():
        @pl.when(z % 4 == dy)
        def _():
            own_w1.start()
            loop(15, lambda i: w1_first(i).start())

        def wait_first():
            @pl.when(z % 4 == dy)
            def _():
                loop(15, lambda i: w1_first(i).wait_send())

        sent.append(wait_first)

    def w1_middle():
        @pl.when(z % 4 == dy)
        def _():
            own_w1.wait()
            drain(w1.at[0, pl.ds(0, 3), 0, 0], w1_sem.at[1])

        @pl.when(z % 4 != dy)
        def _():
            drain(w1.at[0, :, 0, 0], w1_sem.at[1])

        loop(15, lambda i: w1_second(i).start())
        sent.append(lambda: drain(tiles_hbm.at[pl.ds(0, 240)], w1_sem.at[2]))

    def w1_last():
        drain(tiles_hbm.at[pl.ds(0, 240)], w1_sem.at[3])
        w1_third.start()

    def w1_end():
        w1_third.wait()

    def scorer(b):
        part = pl.ds(b * BLOCK, BLOCK)
        x = tiles[part, :]
        if b == 0:
            loads[0].wait()
        tanh_part = jnp.tanh(matmul(x, wv[...]))
        if b == 0:
            loads[1].wait()
            small[0].wait()
        gate_part = 0.5 + 0.5 * jnp.tanh(0.5 * matmul(x, wu[...]))
        low = (tanh_part * gate_part).astype(bf16)
        gated[part, :] = low
        scores[:, part] = matmul(sw[...], low, NT)

    for b in range(rows // BLOCK):
        if b == 2:
            pl.semaphore_wait(barrier, 46)
            w1_start()
        loads[2 + b].wait()
        scorer(b)
    for load in small[1:]:
        load.wait()

    member = lax.broadcasted_iota(jnp.int32, (16, rows), 0) == seg[...]
    lane = lax.broadcasted_iota(jnp.int32, (16, 128), 1)
    top = jnp.full((16, 128), LOW, f32)
    total = jnp.zeros((16, 128), f32)
    for k in range(8):
        score = jnp.broadcast_to(scores[k : k + 1, :], (16, rows))
        peak = jnp.max(jnp.where(member, score, LOW), axis=1, keepdims=True)
        term = jnp.where(member, jnp.exp(score - peak), 0.0)
        expo[16 * k : 16 * k + 16, :] = term
        top = jnp.where(lane == k, peak, top)
        total = jnp.where(lane == k, jnp.sum(term, axis=1, keepdims=True), total)

    blocks = []
    for q in range(4):
        upper, lower = split(expo[32 * q : 32 * q + 32, :])
        both = matmul(jnp.concatenate([upper, lower], axis=0), tiles[:, 384 * q : 384 * q + 384])
        both = both[:32] + both[32:]
        first, second = both[:16], both[16:]
        blocks += [
            first[:, :128],
            jnp.where(lane < 64, first[:, 128:256], second[:, 128:256]),
            second[:, 256:],
        ]

    def pick(a, b):
        return jnp.where(c == 0, a, b)

    def strided(j):
        return pl.ds(j, 16, stride=8)

    for j in range(6):
        swap_out[strided(j), :] = pick(blocks[6 + j], blocks[j])
    swap_out[strided(6), :] = total
    swap_out[strided(7), :] = top
    swap = remote(swap_out, swap_in, half_sem.at[0], half_sem.at[1], tile=other_t)
    swap.start()
    mine = [pick(blocks[j], blocks[6 + j]) for j in range(6)]
    swap.wait()

    low_lane = lane < 64

    def spread(table):
        heads = [pick(table[:, k : k + 1], table[:, 4 + k : 5 + k]) for k in range(4)]
        n = table.shape[0]
        heads = [jnp.broadcast_to(h, (n, 128)) for h in heads]
        low = low_lane[:n]
        return [
            heads[0], jnp.where(low, heads[0], heads[1]), heads[1],
            heads[2], jnp.where(low, heads[2], heads[3]), heads[3],
        ]

    top_other = swap_in[strided(7), :]
    pair_top = jnp.maximum(top, top_other)
    scale, scale_other = jnp.exp(top - pair_top), jnp.exp(top_other - pair_top)
    wide_own, wide_other = spread(scale), spread(scale_other)
    for j in range(6):
        red_out[strided(j), :] = mine[j] * wide_own[j] + swap_in[strided(j), :] * wide_other[j]
    red_out[strided(6), :] = total * scale + swap_in[strided(6), :] * scale_other
    red_out[strided(7), :] = pair_top

    def eight(i):
        return pl.ds(pl.multiple_of(8 * i, 8), 8)

    def reduce_copy(i):
        return remote(red_out.at[eight(z_place(i))], red_in.at[eight(z)], red_sem.at[0], red_sem.at[1], **z_peer(i))

    loop(15, lambda i: reduce_copy(i).start())
    sent.append(lambda: drain(red_in.at[pl.ds(0, 120)], red_sem.at[0]))
    red_in[eight(z), :] = red_out[eight(z), :]

    w1_middle()

    drain(red_in.at[pl.ds(0, 120)], red_sem.at[1])
    tops = red_in[strided(7), :]
    slide_top = jnp.max(tops, axis=0, keepdims=True)
    scale = jnp.exp(tops - slide_top)
    slide_total = jnp.sum(red_in[strided(6), :] * scale, axis=0, keepdims=True)
    wide_scale, wide_total = spread(scale), spread(slide_total)
    tile_rows = [
        jnp.sum(red_in[strided(j), :] * wide_scale[j], axis=0, keepdims=True) / wide_total[j]
        for j in range(6)
    ]
    own_half[eight(z), :] = jnp.concatenate(tile_rows + [slide_total, slide_top], axis=0)

    def gather_copy(i):
        return remote(own_half.at[eight(z)], own_half.at[eight(z)], all_sem.at[0], all_sem.at[1], **z_peer(i))

    loop(15, lambda i: gather_copy(i).start())
    sent.append(lambda: drain(own_half.at[pl.ds(0, 120)], all_sem.at[0]))
    w1_last()
    drain(own_half.at[pl.ds(0, 120)], all_sem.at[1])
    relay = remote(own_half, other_half, half_sem.at[2], half_sem.at[3], tile=other_t)
    relay.start()
    w1_end()
    relay.wait()

    left, right = [], []
    for j in range(6):
        a, b = own_half[strided(j), :], other_half[strided(j), :]
        left.append(pick(a, b))
        right.append(pick(b, a))
    pooled = jnp.concatenate(left + right, axis=1)
    slide_total, slide_top = own_half[strided(6), :], own_half[strided(7), :]
    width = pooled.shape[1]
    root_mean = jnp.sqrt(jnp.sum(pooled * pooled, axis=1, keepdims=True) / width + 1e-5)
    normed = pooled / root_mean
    normed_low = normed.astype(bf16)
    whole = jnp.concatenate([w1[x].reshape(width, 128) for x in range(4)], axis=1)
    pre_act = matmul(normed_low, whole)
    phi = 0.5 * (1.0 + lax.erf(pre_act * 0.7071067811865476))
    hidden = pre_act * phi
    w2_float = w2[...].astype(f32).reshape(1, pre_act.shape[1])
    logits = jnp.sum(hidden * w2_float, axis=1, keepdims=True)
    square = lax.broadcasted_iota(jnp.int32, (16, 16), 0) == lax.broadcasted_iota(jnp.int32, (16, 16), 1)
    target = jnp.sum(
        jnp.where(square, jnp.broadcast_to(lab[...], (16, 16)).astype(f32), 0.0), axis=1, keepdims=True
    )
    soft = jnp.exp(-jnp.abs(logits))
    loss_part = jnp.sum(jnp.maximum(logits, 0.0) + jnp.log1p(soft) - target * logits, axis=0, keepdims=True)
    logit_grad = jnp.where(logits >= 0.0, 1.0, soft) / (1.0 + soft) - target
    w2_part = jnp.sum(logit_grad * hidden, axis=0, keepdims=True)
    pre_grad = logit_grad * w2_float * gelu_slope(pre_act, phi)

    upper, lower = split(pre_grad)
    both = matmul(jnp.concatenate([upper, lower], axis=0), whole, NT)
    norm_grad = both[:16] + both[16:]
    pool_grad = (norm_grad - normed * (jnp.sum(norm_grad * normed, axis=1, keepdims=True) / width)) / root_mean

    product = pooled * pool_grad
    weight = jnp.exp(top - slide_top) / slide_total
    lane_pair = lax.broadcasted_iota(jnp.int32, (16, 384), 1)
    for q in range(4):
        grads = pool_grad[:, 384 * q : 384 * q + 384]
        terms = product[:, 384 * q : 384 * q + 384]
        pair = jnp.concatenate(
            [jnp.where(lane_pair < 192, grads, 0.0), jnp.where(lane_pair >= 192, grads, 0.0)], axis=0
        )
        upper, lower = split(pair)
        both = matmul(jnp.concatenate([upper, lower], axis=0), tiles[:, 384 * q : 384 * q + 384], NT)
        both = both[:32] + both[32:]
        for half in range(2):
            k = 2 * q + half
            side = lane_pair < 192 if half == 0 else lane_pair >= 192
            inner = jnp.sum(jnp.where(side, terms, 0.0), axis=1, keepdims=True)
            change = expo[16 * k : 16 * k + 16, :] * ((both[16 * half : 16 * half + 16] - inner) * weight[:, k : k + 1])
            delta[k : k + 1, :] = jnp.sum(change, axis=0, keepdims=True)

    upper, lower = split(delta[...])
    both = matmul(jnp.concatenate([upper, lower], axis=0), gated[...])
    score_part = both[:8] + both[8:]

    part, rest = score_part[:, :256], score_part[:, 256:]
    gs_out[...] = pick(rest, part)
    gs_swap = remote(gs_out, gs_in, gs_sem.at[0], gs_sem.at[1], tile=other_t)
    gs_swap.start()
    part = pick(part, rest)

    wide[:, :width] = normed_low.astype(f32)
    wide[:, width:] = jnp.zeros((16, 128), f32)
    first = 48 * t
    window = wide[:, pl.ds(pl.multiple_of(first // 128 * 128, 128), 256)].astype(bf16)
    chosen = lax.broadcasted_iota(jnp.int32, (256, 128), 0) == (
        lax.broadcasted_iota(jnp.int32, (256, 128), 1) + first % 128
    )
    normed_own = matmul(window, jnp.where(chosen, 1.0, 0.0).astype(bf16))
    sub = lax.broadcasted_iota(jnp.int32, (16, 128), 0)
    extra = jnp.zeros((16, 128), f32)
    for j in range(5):
        piece = w2_part[:, 128 * j : 128 * j + 128] if j < 4 else jnp.broadcast_to(loss_part, (1, 128))
        upper = piece.astype(bf16).astype(f32)
        extra = jnp.where(sub == j, upper, extra)
        extra = jnp.where(sub == 8 + j, piece - upper, extra)
    msg[d] = jnp.concatenate([pre_grad, normed_own, extra], axis=1).astype(bf16)

    def message(i):
        return remote(msg.at[d], msg.at[d], msg_sem.at[0], msg_sem.at[1], **dp_peer(i))

    loop(15, lambda i: message(i).start())
    sent.append(lambda: drain(msg.at[pl.ds(0, 15)], msg_sem.at[0]))
    gs_swap.wait()
    part = part + gs_in[...]

    gz[z] = jnp.concatenate([part[:, :128], part[:, 128:]], axis=0).astype(bf16)

    def gs_z(i):
        return remote(gz.at[z], gz.at[z], gz_sem.at[0], gz_sem.at[1], **z_peer(i))

    loop(15, lambda i: gs_z(i).start())
    sent.append(lambda: drain(gz.at[pl.ds(0, 15)], gz_sem.at[0]))

    drain(gz.at[pl.ds(0, 15)], gz_sem.at[1])

    ga[place] = jnp.sum(gz[...].astype(f32), axis=0).astype(bf16)

    def gs_plane(i):
        return remote(ga.at[place], ga.at[place], ga_sem.at[0], ga_sem.at[1], **plane_peer(i))

    loop(31, lambda i: gs_plane(i).start())
    sent.append(lambda: drain(ga.at[pl.ds(0, 31)], ga_sem.at[0]))
    drain(msg.at[pl.ds(0, 15)], msg_sem.at[1])
    grads = msg[:, :, 0:512].reshape(256, 512)
    own = msg[:, :, 512:640].reshape(256, 128)
    gw1_ref[...] = matmul(own, grads, TN)[:48]
    sums = jnp.sum(msg[:, :, 640:768].astype(f32), axis=0)
    sums = sums[:8] + sums[8:]
    gw2_ref[...] = jnp.concatenate([sums[j : j + 1] for j in range(4)], axis=1)
    loss_ref[...] = sums[4:5, 0:1] * (1.0 / 256.0)

    drain(ga.at[pl.ds(0, 31)], ga_sem.at[1])
    parts = ga[...].astype(f32).reshape(16, 2, 16, 128)
    for half in range(2):
        sums = jnp.sum(parts[:, half], axis=0)
        gs_ref[:, 256 * half : 256 * half + 128] = sums[:8]
        gs_ref[:, 256 * half + 128 : 256 * half + 256] = sums[8:]

    finish()


def body(tiles, slide_of_tile, labels, attn_v, attn_u, score_w, head_w1, head_w2):
    rows, width = tiles.shape
    hid = attn_v.shape[1]
    vmem, hbm = pl.BlockSpec(memory_space=pltpu.VMEM), pl.BlockSpec(memory_space=pltpu.HBM)
    dma = pltpu.SemaphoreType.DMA
    shapes = tuple(jax.ShapeDtypeStruct(shape, f32) for shape in ((48, hid), (8, hid), (1, hid), (1, 1)))
    results = pl.pallas_call(
        kernel,
        out_shape=tuple(pltpu.VMEM(x.shape, f32) for x in shapes),
        in_specs=[hbm] * 8,
        out_specs=(vmem, vmem, vmem, vmem),
        scratch_shapes=[
            pltpu.VMEM((rows, width), bf16),
            pltpu.VMEM((1, rows), jnp.int32),
            pltpu.VMEM((1, 16), jnp.int32),
            pltpu.VMEM((width, hid), bf16),
            pltpu.VMEM((width, hid), bf16),
            pltpu.VMEM((8, hid), bf16),
            pltpu.VMEM((hid,), bf16),
            pltpu.VMEM((rows, hid), bf16),
            pltpu.VMEM((8, rows), f32),
            pltpu.VMEM((128, rows), f32),
            pltpu.VMEM((4, 4, 4, 2, 48, 128), bf16),
            pltpu.VMEM((8, rows), f32),
            pltpu.VMEM((128, 128), f32),
            pltpu.VMEM((128, 128), f32),
            pltpu.VMEM((128, 128), f32),
            pltpu.VMEM((128, 128), f32),
            pltpu.VMEM((128, 128), f32),
            pltpu.VMEM((128, 128), f32),
            pltpu.VMEM((16, width + 128), f32),
            pltpu.VMEM((16, 16, 768), bf16),
            pltpu.VMEM((8, 256), f32),
            pltpu.VMEM((8, 256), f32),
            pltpu.VMEM((16, 16, 128), bf16),
            pltpu.VMEM((32, 16, 128), bf16),
            dma((12,)), dma((6,)), dma((4,)), dma((2,)), dma((2,)), dma((2,)), dma((2,)), dma((2,)), dma((2,)),
        ],
        compiler_params=pltpu.CompilerParams(
            collective_id=0, has_side_effects=True, vmem_limit_bytes=60 * 1024 * 1024
        ),
    )(tiles, slide_of_tile, labels, attn_v, attn_u, score_w.T, head_w1, head_w2)
    grad_w1, grad_score, grad_w2, loss = results
    return grad_w1, grad_score.T, grad_w2.reshape(hid), loss.reshape(())


def solution(mesh):
    return jax.shard_map(
        body,
        mesh=mesh,
        in_specs=(
            P(("dp", "tile"), None),
            P("dp", "tile"),
            P("dp", None),
            P(),
            P(),
            P(),
            P("tile", None),
            P(),
        ),
        out_specs=(P("tile", None), P(), P(), P()),
        check_vma=False,
    )
```

```python
import functools

import jax
import jax.numpy as jnp
from jax import lax
from jax.experimental import pallas as pl
from jax.experimental.pallas import tpu as pltpu
from jax.sharding import PartitionSpec as P

f32, bf16 = jnp.float32, jnp.bfloat16
MESH = pl.DeviceIdType.MESH
LOW = -3.0e38
BLOCK = 256
NN = (((1,), (0,)), ((), ()))
NT = (((1,), (1,)), ((), ()))
TN = (((0,), (0,)), ((), ()))


def matmul(a, b, dims=NN):
    return lax.dot_general(a, b, dims, preferred_element_type=f32)


def split(values):
    upper = values.astype(bf16)
    return upper, (values - upper.astype(f32)).astype(bf16)


def gelu_slope(values, phi):
    return phi + values * jnp.exp(-0.5 * values * values) * 0.3989422804014327


def remote(src, dst, send, recv, **where):
    return pltpu.make_async_remote_copy(
        src_ref=src, dst_ref=dst, send_sem=send, recv_sem=recv,
        device_id=where, device_id_type=MESH,
    )


def drain(ref, sem):
    pltpu.make_async_copy(ref, ref, sem).wait()


def kernel(
    tiles_hbm, seg_hbm, lab_hbm, v_hbm, u_hbm, sw_hbm, w1_hbm, w2_hbm,
    gw1_ref, gs_ref, gw2_ref, loss_ref,
    tiles, seg, lab, wv, wu, sw, w2,
    gated, scores, expo, w1, delta,
    swap_out, swap_in, red_out, red_in, own_half, other_half,
    wide, msg, gs_out, gs_in, gz, ga,
    load_sem, w1_sem, half_sem, red_sem, all_sem, msg_sem, gs_sem, gz_sem, ga_sem,
):
    d, t = lax.axis_index("dp"), lax.axis_index("tile")
    z, c = t // 2, t % 2
    other_t = 2 * z + 1 - c
    dx, dy = d // 4, d % 4
    rows = tiles.shape[0]
    sent = []

    def finish():
        for wait in sent:
            wait()

    def loop(count, step):
        def go(i, carry):
            step(i)
            return carry

        lax.fori_loop(0, count, go, 0)

    barrier = pltpu.get_barrier_semaphore()

    place = 2 * d + c

    def turn(i):
        return 2 + 3 * i + 3 * (i * (i - 1) // 2)

    def dp_peer(i):
        return {"dp": (dx + turn(i // 4)) % 4 * 4 + (dy + turn(i % 4)) % 4}

    def plane_peer(i):
        return {**dp_peer(i // 2), "tile": 2 * z + (c + 1 + i) % 2}

    def z_place(i):
        return (z + 8 + (1 - 2 * (i % 2)) * ((i + 1) // 2)) % 16

    def z_peer(i):
        return {"tile": 2 * z_place(i) + c}

    def greet(who):
        pl.semaphore_signal(barrier, inc=1, device_id=who, device_id_type=MESH)

    loop(15, lambda i: greet(z_peer(i)))

    loads = [
        pltpu.make_async_copy(v_hbm, wv, load_sem.at[0]),
        pltpu.make_async_copy(u_hbm, wu, load_sem.at[1]),
    ]
    for b in range(rows // BLOCK):
        part = pl.ds(b * BLOCK, BLOCK)
        loads.append(pltpu.make_async_copy(tiles_hbm.at[part], tiles.at[part], load_sem.at[2 + b]))
    small = [
        pltpu.make_async_copy(sw_hbm, sw, load_sem.at[8]),
        pltpu.make_async_copy(seg_hbm, seg, load_sem.at[9]),
        pltpu.make_async_copy(lab_hbm, lab, load_sem.at[10]),
        pltpu.make_async_copy(w2_hbm, w2, load_sem.at[11]),
    ]
    own_w1 = pltpu.make_async_copy(
        w1_hbm.at[:, pl.ds(pl.multiple_of(dx * 128, 128), 128)],
        w1.at[dx, z // 4, z % 4, c], load_sem.at[7],
    )
    for load in [loads[2], *loads[:2], small[0], *loads[3:], *small[1:]]:
        load.start()

    loop(31, lambda i: greet(plane_peer(i)))


    def w1_first(i):
        return remote(
            w1_hbm.at[:, pl.ds(pl.multiple_of(dx * 128, 128), 128)],
            w1.at[dx, z // 4, z % 4, c], w1_sem.at[0], w1_sem.at[1], **z_peer(i),
        )

    def w1_second(i):
        part = w1.at[dx, :, dy, c]
        return remote(part, part, w1_sem.at[2], w1_sem.at[3], **dp_peer(i))

    w1_third = remote(w1.at[:, :, :, c], w1.at[:, :, :, c], w1_sem.at[4], w1_sem.at[5], tile=other_t)

    def w1_start():
        @pl.when(z % 4 == dy)
        def _():
            own_w1.start()
            loop(15, lambda i: w1_first(i).start())

        def wait_first():
            @pl.when(z % 4 == dy)
            def _():
                loop(15, lambda i: w1_first(i).wait_send())

        sent.append(wait_first)

    def w1_middle():
        @pl.when(z % 4 == dy)
        def _():
            own_w1.wait()
            drain(w1.at[0, pl.ds(0, 3), 0, 0], w1_sem.at[1])

        @pl.when(z % 4 != dy)
        def _():
            drain(w1.at[0, :, 0, 0], w1_sem.at[1])

        loop(15, lambda i: w1_second(i).start())
        sent.append(lambda: drain(tiles_hbm.at[pl.ds(0, 240)], w1_sem.at[2]))

    def w1_last():
        drain(tiles_hbm.at[pl.ds(0, 240)], w1_sem.at[3])
        w1_third.start()

    def w1_end():
        w1_third.wait()

    def scorer(b):
        part = pl.ds(b * BLOCK, BLOCK)
        x = tiles[part, :]
        if b == 0:
            loads[0].wait()
        tanh_part = jnp.tanh(matmul(x, wv[...]))
        if b == 0:
            loads[1].wait()
            small[0].wait()
        gate_part = 0.5 + 0.5 * jnp.tanh(0.5 * matmul(x, wu[...]))
        low = (tanh_part * gate_part).astype(bf16)
        gated[part, :] = low
        scores[:, part] = matmul(sw[...], low, NT)

    for b in range(rows // BLOCK):
        if b == 2:
            pl.semaphore_wait(barrier, 46)
            w1_start()
        loads[2 + b].wait()
        scorer(b)
    for load in small[1:]:
        load.wait()

    member = lax.broadcasted_iota(jnp.int32, (16, rows), 0) == seg[...]
    lane = lax.broadcasted_iota(jnp.int32, (16, 128), 1)
    top = jnp.full((16, 128), LOW, f32)
    total = jnp.zeros((16, 128), f32)
    for k in range(8):
        score = jnp.broadcast_to(scores[k : k + 1, :], (16, rows))
        peak = jnp.max(jnp.where(member, score, LOW), axis=1, keepdims=True)
        term = jnp.where(member, jnp.exp(score - peak), 0.0)
        expo[16 * k : 16 * k + 16, :] = term
        top = jnp.where(lane == k, peak, top)
        total = jnp.where(lane == k, jnp.sum(term, axis=1, keepdims=True), total)

    blocks = []
    for q in range(4):
        upper, lower = split(expo[32 * q : 32 * q + 32, :])
        both = matmul(jnp.concatenate([upper, lower], axis=0), tiles[:, 384 * q : 384 * q + 384])
        both = both[:32] + both[32:]
        first, second = both[:16], both[16:]
        blocks += [
            first[:, :128],
            jnp.where(lane < 64, first[:, 128:256], second[:, 128:256]),
            second[:, 256:],
        ]

    def pick(a, b):
        return jnp.where(c == 0, a, b)

    def strided(j):
        return pl.ds(j, 16, stride=8)

    for j in range(6):
        swap_out[strided(j), :] = pick(blocks[6 + j], blocks[j])
    swap_out[strided(6), :] = total
    swap_out[strided(7), :] = top
    swap = remote(swap_out, swap_in, half_sem.at[0], half_sem.at[1], tile=other_t)
    swap.start()
    mine = [pick(blocks[j], blocks[6 + j]) for j in range(6)]
    swap.wait()

    low_lane = lane < 64

    def spread(table):
        heads = [pick(table[:, k : k + 1], table[:, 4 + k : 5 + k]) for k in range(4)]
        n = table.shape[0]
        heads = [jnp.broadcast_to(h, (n, 128)) for h in heads]
        low = low_lane[:n]
        return [
            heads[0], jnp.where(low, heads[0], heads[1]), heads[1],
            heads[2], jnp.where(low, heads[2], heads[3]), heads[3],
        ]

    top_other = swap_in[strided(7), :]
    pair_top = jnp.maximum(top, top_other)
    scale, scale_other = jnp.exp(top - pair_top), jnp.exp(top_other - pair_top)
    wide_own, wide_other = spread(scale), spread(scale_other)
    for j in range(6):
        red_out[strided(j), :] = mine[j] * wide_own[j] + swap_in[strided(j), :] * wide_other[j]
    red_out[strided(6), :] = total * scale + swap_in[strided(6), :] * scale_other
    red_out[strided(7), :] = pair_top

    def eight(i):
        return pl.ds(pl.multiple_of(8 * i, 8), 8)

    def reduce_copy(i):
        return remote(red_out.at[eight(z_place(i))], red_in.at[eight(z)], red_sem.at[0], red_sem.at[1], **z_peer(i))

    loop(15, lambda i: reduce_copy(i).start())
    sent.append(lambda: drain(red_in.at[pl.ds(0, 120)], red_sem.at[0]))
    red_in[eight(z), :] = red_out[eight(z), :]

    w1_middle()

    drain(red_in.at[pl.ds(0, 120)], red_sem.at[1])
    tops = red_in[strided(7), :]
    slide_top = jnp.max(tops, axis=0, keepdims=True)
    scale = jnp.exp(tops - slide_top)
    slide_total = jnp.sum(red_in[strided(6), :] * scale, axis=0, keepdims=True)
    wide_scale, wide_total = spread(scale), spread(slide_total)
    tile_rows = [
        jnp.sum(red_in[strided(j), :] * wide_scale[j], axis=0, keepdims=True) / wide_total[j]
        for j in range(6)
    ]
    own_half[eight(z), :] = jnp.concatenate(tile_rows + [slide_total, slide_top], axis=0)

    def gather_copy(i):
        return remote(own_half.at[eight(z)], own_half.at[eight(z)], all_sem.at[0], all_sem.at[1], **z_peer(i))

    loop(15, lambda i: gather_copy(i).start())
    sent.append(lambda: drain(own_half.at[pl.ds(0, 120)], all_sem.at[0]))
    w1_last()
    drain(own_half.at[pl.ds(0, 120)], all_sem.at[1])
    relay = remote(own_half, other_half, half_sem.at[2], half_sem.at[3], tile=other_t)
    relay.start()
    w1_end()
    relay.wait()

    left, right = [], []
    for j in range(6):
        a, b = own_half[strided(j), :], other_half[strided(j), :]
        left.append(pick(a, b))
        right.append(pick(b, a))
    pooled = jnp.concatenate(left + right, axis=1)
    slide_total, slide_top = own_half[strided(6), :], own_half[strided(7), :]
    width = pooled.shape[1]
    root_mean = jnp.sqrt(jnp.sum(pooled * pooled, axis=1, keepdims=True) / width + 1e-5)
    normed = pooled / root_mean
    normed_low = normed.astype(bf16)
    whole = jnp.concatenate([w1[x].reshape(width, 128) for x in range(4)], axis=1)
    pre_act = matmul(normed_low, whole)
    phi = 0.5 * (1.0 + lax.erf(pre_act * 0.7071067811865476))
    hidden = pre_act * phi
    w2_float = w2[...].astype(f32).reshape(1, pre_act.shape[1])
    logits = jnp.sum(hidden * w2_float, axis=1, keepdims=True)
    square = lax.broadcasted_iota(jnp.int32, (16, 16), 0) == lax.broadcasted_iota(jnp.int32, (16, 16), 1)
    target = jnp.sum(
        jnp.where(square, jnp.broadcast_to(lab[...], (16, 16)).astype(f32), 0.0), axis=1, keepdims=True
    )
    soft = jnp.exp(-jnp.abs(logits))
    loss_part = jnp.sum(jnp.maximum(logits, 0.0) + jnp.log1p(soft) - target * logits, axis=0, keepdims=True)
    logit_grad = jnp.where(logits >= 0.0, 1.0, soft) / (1.0 + soft) - target
    w2_part = jnp.sum(logit_grad * hidden, axis=0, keepdims=True)
    pre_grad = logit_grad * w2_float * gelu_slope(pre_act, phi)

    upper, lower = split(pre_grad)
    both = matmul(jnp.concatenate([upper, lower], axis=0), whole, NT)
    norm_grad = both[:16] + both[16:]
    pool_grad = (norm_grad - normed * (jnp.sum(norm_grad * normed, axis=1, keepdims=True) / width)) / root_mean

    product = pooled * pool_grad
    weight = jnp.exp(top - slide_top) / slide_total
    lane_pair = lax.broadcasted_iota(jnp.int32, (16, 384), 1)
    for q in range(4):
        grads = pool_grad[:, 384 * q : 384 * q + 384]
        terms = product[:, 384 * q : 384 * q + 384]
        pair = jnp.concatenate(
            [jnp.where(lane_pair < 192, grads, 0.0), jnp.where(lane_pair >= 192, grads, 0.0)], axis=0
        )
        upper, lower = split(pair)
        both = matmul(jnp.concatenate([upper, lower], axis=0), tiles[:, 384 * q : 384 * q + 384], NT)
        both = both[:32] + both[32:]
        for half in range(2):
            k = 2 * q + half
            side = lane_pair < 192 if half == 0 else lane_pair >= 192
            inner = jnp.sum(jnp.where(side, terms, 0.0), axis=1, keepdims=True)
            change = expo[16 * k : 16 * k + 16, :] * ((both[16 * half : 16 * half + 16] - inner) * weight[:, k : k + 1])
            delta[k : k + 1, :] = jnp.sum(change, axis=0, keepdims=True)

    upper, lower = split(delta[...])
    both = matmul(jnp.concatenate([upper, lower], axis=0), gated[...])
    score_part = both[:8] + both[8:]

    part, rest = score_part[:, :256], score_part[:, 256:]
    gs_out[...] = pick(rest, part)
    gs_swap = remote(gs_out, gs_in, gs_sem.at[0], gs_sem.at[1], tile=other_t)
    gs_swap.start()
    part = pick(part, rest)

    wide[:, :width] = normed_low.astype(f32)
    wide[:, width:] = jnp.zeros((16, 128), f32)
    first = 48 * t
    window = wide[:, pl.ds(pl.multiple_of(first // 128 * 128, 128), 256)].astype(bf16)
    chosen = lax.broadcasted_iota(jnp.int32, (256, 128), 0) == (
        lax.broadcasted_iota(jnp.int32, (256, 128), 1) + first % 128
    )
    normed_own = matmul(window, jnp.where(chosen, 1.0, 0.0).astype(bf16))
    sub = lax.broadcasted_iota(jnp.int32, (16, 128), 0)
    extra = jnp.zeros((16, 128), f32)
    for j in range(5):
        piece = w2_part[:, 128 * j : 128 * j + 128] if j < 4 else jnp.broadcast_to(loss_part, (1, 128))
        upper = piece.astype(bf16).astype(f32)
        extra = jnp.where(sub == j, upper, extra)
        extra = jnp.where(sub == 8 + j, piece - upper, extra)
    msg[d] = jnp.concatenate([pre_grad, normed_own, extra], axis=1).astype(bf16)

    def message(i):
        return remote(msg.at[d], msg.at[d], msg_sem.at[0], msg_sem.at[1], **dp_peer(i))

    loop(15, lambda i: message(i).start())
    sent.append(lambda: drain(msg.at[pl.ds(0, 15)], msg_sem.at[0]))
    gs_swap.wait()
    part = part + gs_in[...]

    gz[z] = jnp.concatenate([part[:, :128], part[:, 128:]], axis=0).astype(bf16)

    def gs_z(i):
        return remote(gz.at[z], gz.at[z], gz_sem.at[0], gz_sem.at[1], **z_peer(i))

    loop(15, lambda i: gs_z(i).start())
    sent.append(lambda: drain(gz.at[pl.ds(0, 15)], gz_sem.at[0]))

    drain(gz.at[pl.ds(0, 15)], gz_sem.at[1])

    ga[place] = jnp.sum(gz[...].astype(f32), axis=0).astype(bf16)

    def gs_plane(i):
        return remote(ga.at[place], ga.at[place], ga_sem.at[0], ga_sem.at[1], **plane_peer(i))

    loop(31, lambda i: gs_plane(i).start())
    sent.append(lambda: drain(ga.at[pl.ds(0, 31)], ga_sem.at[0]))
    drain(msg.at[pl.ds(0, 15)], msg_sem.at[1])
    grads = msg[:, :, 0:512].reshape(256, 512)
    own = msg[:, :, 512:640].reshape(256, 128)
    gw1_ref[...] = matmul(own, grads, TN)[:48]
    sums = jnp.sum(msg[:, :, 640:768].astype(f32), axis=0)
    sums = sums[:8] + sums[8:]
    gw2_ref[...] = jnp.concatenate([sums[j : j + 1] for j in range(4)], axis=1)
    loss_ref[...] = sums[4:5, 0:1] * (1.0 / 256.0)

    drain(ga.at[pl.ds(0, 31)], ga_sem.at[1])
    parts = ga[...].astype(f32).reshape(16, 2, 16, 128)
    for half in range(2):
        sums = jnp.sum(parts[:, half], axis=0)
        gs_ref[:, 256 * half : 256 * half + 128] = sums[:8]
        gs_ref[:, 256 * half + 128 : 256 * half + 256] = sums[8:]

    finish()


def body(tiles, slide_of_tile, labels, attn_v, attn_u, score_w, head_w1, head_w2):
    rows, width = tiles.shape
    hid = attn_v.shape[1]
    vmem, hbm = pl.BlockSpec(memory_space=pltpu.VMEM), pl.BlockSpec(memory_space=pltpu.HBM)
    dma = pltpu.SemaphoreType.DMA
    shapes = tuple(jax.ShapeDtypeStruct(shape, f32) for shape in ((48, hid), (8, hid), (1, hid), (1, 1)))
    results = pl.pallas_call(
        kernel,
        out_shape=tuple(pltpu.VMEM(x.shape, f32) for x in shapes),
        in_specs=[hbm] * 8,
        out_specs=(vmem, vmem, vmem, vmem),
        scratch_shapes=[
            pltpu.VMEM((rows, width), bf16),
            pltpu.VMEM((1, rows), jnp.int32),
            pltpu.VMEM((1, 16), jnp.int32),
            pltpu.VMEM((width, hid), bf16),
            pltpu.VMEM((width, hid), bf16),
            pltpu.VMEM((8, hid), bf16),
            pltpu.VMEM((hid,), bf16),
            pltpu.VMEM((rows, hid), bf16),
            pltpu.VMEM((8, rows), f32),
            pltpu.VMEM((128, rows), f32),
            pltpu.VMEM((4, 4, 4, 2, 48, 128), bf16),
            pltpu.VMEM((8, rows), f32),
            pltpu.VMEM((128, 128), f32),
            pltpu.VMEM((128, 128), f32),
            pltpu.VMEM((128, 128), f32),
            pltpu.VMEM((128, 128), f32),
            pltpu.VMEM((128, 128), f32),
            pltpu.VMEM((128, 128), f32),
            pltpu.VMEM((16, width + 128), f32),
            pltpu.VMEM((16, 16, 768), bf16),
            pltpu.VMEM((8, 256), f32),
            pltpu.VMEM((8, 256), f32),
            pltpu.VMEM((16, 16, 128), bf16),
            pltpu.VMEM((32, 16, 128), bf16),
            dma((12,)), dma((6,)), dma((4,)), dma((2,)), dma((2,)), dma((2,)), dma((2,)), dma((2,)), dma((2,)),
        ],
        compiler_params=pltpu.CompilerParams(
            collective_id=0, has_side_effects=True, vmem_limit_bytes=60 * 1024 * 1024
        ),
    )(tiles, slide_of_tile, labels, attn_v, attn_u, score_w.T, head_w1, head_w2)
    grad_w1, grad_score, grad_w2, loss = results
    return grad_w1, grad_score.T, grad_w2.reshape(hid), loss.reshape(())


def solution(mesh):
    return jax.shard_map(
        body,
        mesh=mesh,
        in_specs=(
            P(("dp", "tile"), None),
            P("dp", "tile"),
            P("dp", None),
            P(),
            P(),
            P(),
            P("tile", None),
            P(),
        ),
        out_specs=(P("tile", None), P(), P(), P()),
        check_vma=False,
    )
```

```python
import functools

import jax
import jax.numpy as jnp
from jax import lax
from jax.experimental import pallas as pl
from jax.experimental.pallas import tpu as pltpu
from jax.sharding import PartitionSpec as P

f32, bf16 = jnp.float32, jnp.bfloat16
MESH = pl.DeviceIdType.MESH
LOW = -3.0e38
BLOCK = 256
NN = (((1,), (0,)), ((), ()))
NT = (((1,), (1,)), ((), ()))
TN = (((0,), (0,)), ((), ()))


def matmul(a, b, dims=NN):
    return lax.dot_general(a, b, dims, preferred_element_type=f32)


def split(values):
    upper = values.astype(bf16)
    return upper, (values - upper.astype(f32)).astype(bf16)


def gelu_slope(values, phi):
    return phi + values * jnp.exp(-0.5 * values * values) * 0.3989422804014327


def remote(src, dst, send, recv, **where):
    return pltpu.make_async_remote_copy(
        src_ref=src, dst_ref=dst, send_sem=send, recv_sem=recv,
        device_id=where, device_id_type=MESH,
    )


def drain(ref, sem):
    pltpu.make_async_copy(ref, ref, sem).wait()


def kernel(
    tiles_hbm, seg_hbm, lab_hbm, v_hbm, u_hbm, sw_hbm, w1_hbm, w2_hbm,
    gw1_ref, gs_ref, gw2_ref, loss_ref,
    tiles, seg, lab, wv, wu, sw, w2,
    gated, scores, expo, w1, delta,
    swap_out, swap_in, red_out, red_in, own_half, other_half,
    wide, msg, gs_out, gs_in, gz, ga,
    load_sem, w1_sem, half_sem, red_sem, all_sem, msg_sem, gs_sem, gz_sem, ga_sem,
):
    d, t = lax.axis_index("dp"), lax.axis_index("tile")
    z, c = t // 2, t % 2
    other_t = 2 * z + 1 - c
    dx, dy = d // 4, d % 4
    rows = tiles.shape[0]
    sent = []

    def finish():
        for wait in sent:
            wait()

    def loop(count, step):
        def go(i, carry):
            step(i)
            return carry

        lax.fori_loop(0, count, go, 0)

    barrier = pltpu.get_barrier_semaphore()

    place = 2 * d + c

    def turn(i):
        return 2 + 3 * i + 3 * (i * (i - 1) // 2)

    def dp_peer(i):
        return {"dp": (dx + turn(i // 4)) % 4 * 4 + (dy + turn(i % 4)) % 4}

    def plane_peer(i):
        return {**dp_peer(i // 2), "tile": 2 * z + (c + 1 + i) % 2}

    def z_place(i):
        return (z + 8 + (1 - 2 * (i % 2)) * ((i + 1) // 2)) % 16

    def z_peer(i):
        return {"tile": 2 * z_place(i) + c}

    def greet(who):
        pl.semaphore_signal(barrier, inc=1, device_id=who, device_id_type=MESH)

    loop(15, lambda i: greet(z_peer(i)))

    loads = [
        pltpu.make_async_copy(v_hbm, wv, load_sem.at[0]),
        pltpu.make_async_copy(u_hbm, wu, load_sem.at[1]),
    ]
    for b in range(rows // BLOCK):
        part = pl.ds(b * BLOCK, BLOCK)
        loads.append(pltpu.make_async_copy(tiles_hbm.at[part], tiles.at[part], load_sem.at[2 + b]))
    small = [
        pltpu.make_async_copy(sw_hbm, sw, load_sem.at[8]),
        pltpu.make_async_copy(seg_hbm, seg, load_sem.at[9]),
        pltpu.make_async_copy(lab_hbm, lab, load_sem.at[10]),
        pltpu.make_async_copy(w2_hbm, w2, load_sem.at[11]),
    ]
    own_w1 = pltpu.make_async_copy(
        w1_hbm.at[:, pl.ds(pl.multiple_of(dx * 128, 128), 128)],
        w1.at[dx, z // 4, z % 4, c], load_sem.at[7],
    )
    for load in [loads[2], *loads[:2], small[0], *loads[3:], *small[1:]]:
        load.start()

    loop(31, lambda i: greet(plane_peer(i)))


    def w1_first(i):
        return remote(
            w1_hbm.at[:, pl.ds(pl.multiple_of(dx * 128, 128), 128)],
            w1.at[dx, z // 4, z % 4, c], w1_sem.at[0], w1_sem.at[1], **z_peer(i),
        )

    def w1_second(i):
        part = w1.at[dx, :, dy, c]
        return remote(part, part, w1_sem.at[2], w1_sem.at[3], **dp_peer(i))

    w1_third = remote(w1.at[:, :, :, c], w1.at[:, :, :, c], w1_sem.at[4], w1_sem.at[5], tile=other_t)

    def w1_start():
        @pl.when(z % 4 == dy)
        def _():
            own_w1.start()
            loop(15, lambda i: w1_first(i).start())

        def wait_first():
            @pl.when(z % 4 == dy)
            def _():
                loop(15, lambda i: w1_first(i).wait_send())

        sent.append(wait_first)

    def w1_middle():
        @pl.when(z % 4 == dy)
        def _():
            own_w1.wait()
            drain(w1.at[0, pl.ds(0, 3), 0, 0], w1_sem.at[1])

        @pl.when(z % 4 != dy)
        def _():
            drain(w1.at[0, :, 0, 0], w1_sem.at[1])

        loop(15, lambda i: w1_second(i).start())
        sent.append(lambda: drain(tiles_hbm.at[pl.ds(0, 240)], w1_sem.at[2]))

    def w1_last():
        drain(tiles_hbm.at[pl.ds(0, 240)], w1_sem.at[3])
        w1_third.start()

    def w1_end():
        w1_third.wait()

    def scorer(b):
        part = pl.ds(b * BLOCK, BLOCK)
        x = tiles[part, :]
        if b == 0:
            loads[0].wait()
        tanh_part = jnp.tanh(matmul(x, wv[...]))
        if b == 0:
            loads[1].wait()
            small[0].wait()
        gate_part = 0.5 + 0.5 * jnp.tanh(0.5 * matmul(x, wu[...]))
        low = (tanh_part * gate_part).astype(bf16)
        gated[part, :] = low
        scores[:, part] = matmul(sw[...], low, NT)

    for b in range(rows // BLOCK):
        if b == 2:
            pl.semaphore_wait(barrier, 46)
            w1_start()
        loads[2 + b].wait()
        scorer(b)
    for load in small[1:]:
        load.wait()

    member = lax.broadcasted_iota(jnp.int32, (16, rows), 0) == seg[...]
    lane = lax.broadcasted_iota(jnp.int32, (16, 128), 1)
    top = jnp.full((16, 128), LOW, f32)
    total = jnp.zeros((16, 128), f32)
    for k in range(8):
        score = jnp.broadcast_to(scores[k : k + 1, :], (16, rows))
        peak = jnp.max(jnp.where(member, score, LOW), axis=1, keepdims=True)
        term = jnp.where(member, jnp.exp(score - peak), 0.0)
        expo[16 * k : 16 * k + 16, :] = term
        top = jnp.where(lane == k, peak, top)
        total = jnp.where(lane == k, jnp.sum(term, axis=1, keepdims=True), total)

    def pool(half):
        blocks = []
        for i in range(2):
            upper, lower = split(expo[pl.ds(pl.multiple_of(64 * half + 32 * i, 32), 32), :])
            part = tiles[:, pl.ds(pl.multiple_of(768 * half + 384 * i, 128), 384)]
            both = matmul(jnp.concatenate([upper, lower], axis=0), part)
            both = both[:32] + both[32:]
            first, second = both[:16], both[16:]
            blocks += [
                first[:, :128],
                jnp.where(lane < 64, first[:, 128:256], second[:, 128:256]),
                second[:, 256:],
            ]
        return blocks

    def pick(a, b):
        return jnp.where(c == 0, a, b)

    def strided(j):
        return pl.ds(j, 16, stride=8)

    for j, block in enumerate(pool(1 - c)):
        swap_out[strided(j), :] = block
    swap_out[strided(6), :] = total
    swap_out[strided(7), :] = top
    swap = remote(swap_out, swap_in, half_sem.at[0], half_sem.at[1], tile=other_t)
    swap.start()
    mine = pool(c)
    swap.wait()

    low_lane = lane < 64

    def spread(table):
        heads = [pick(table[:, k : k + 1], table[:, 4 + k : 5 + k]) for k in range(4)]
        n = table.shape[0]
        heads = [jnp.broadcast_to(h, (n, 128)) for h in heads]
        low = low_lane[:n]
        return [
            heads[0], jnp.where(low, heads[0], heads[1]), heads[1],
            heads[2], jnp.where(low, heads[2], heads[3]), heads[3],
        ]

    top_other = swap_in[strided(7), :]
    pair_top = jnp.maximum(top, top_other)
    scale, scale_other = jnp.exp(top - pair_top), jnp.exp(top_other - pair_top)
    wide_own, wide_other = spread(scale), spread(scale_other)
    for j in range(6):
        red_out[strided(j), :] = mine[j] * wide_own[j] + swap_in[strided(j), :] * wide_other[j]
    red_out[strided(6), :] = total * scale + swap_in[strided(6), :] * scale_other
    red_out[strided(7), :] = pair_top

    def eight(i):
        return pl.ds(pl.multiple_of(8 * i, 8), 8)

    def reduce_copy(i):
        return remote(red_out.at[eight(z_place(i))], red_in.at[eight(z)], red_sem.at[0], red_sem.at[1], **z_peer(i))

    loop(15, lambda i: reduce_copy(i).start())
    sent.append(lambda: drain(red_in.at[pl.ds(0, 120)], red_sem.at[0]))
    red_in[eight(z), :] = red_out[eight(z), :]

    w1_middle()

    drain(red_in.at[pl.ds(0, 120)], red_sem.at[1])
    tops = red_in[strided(7), :]
    slide_top = jnp.max(tops, axis=0, keepdims=True)
    scale = jnp.exp(tops - slide_top)
    slide_total = jnp.sum(red_in[strided(6), :] * scale, axis=0, keepdims=True)
    wide_scale, wide_total = spread(scale), spread(slide_total)
    tile_rows = [
        jnp.sum(red_in[strided(j), :] * wide_scale[j], axis=0, keepdims=True) / wide_total[j]
        for j in range(6)
    ]
    own_half[eight(z), :] = jnp.concatenate(tile_rows + [slide_total, slide_top], axis=0)

    def gather_copy(i):
        return remote(own_half.at[eight(z)], own_half.at[eight(z)], all_sem.at[0], all_sem.at[1], **z_peer(i))

    loop(15, lambda i: gather_copy(i).start())
    sent.append(lambda: drain(own_half.at[pl.ds(0, 120)], all_sem.at[0]))
    w1_last()
    drain(own_half.at[pl.ds(0, 120)], all_sem.at[1])
    relay = remote(own_half, other_half, half_sem.at[2], half_sem.at[3], tile=other_t)
    relay.start()
    w1_end()
    relay.wait()

    left, right = [], []
    for j in range(6):
        a, b = own_half[strided(j), :], other_half[strided(j), :]
        left.append(pick(a, b))
        right.append(pick(b, a))
    pooled = jnp.concatenate(left + right, axis=1)
    slide_total, slide_top = own_half[strided(6), :], own_half[strided(7), :]
    width = pooled.shape[1]
    root_mean = jnp.sqrt(jnp.sum(pooled * pooled, axis=1, keepdims=True) / width + 1e-5)
    normed = pooled / root_mean
    normed_low = normed.astype(bf16)
    whole = jnp.concatenate([w1[x].reshape(width, 128) for x in range(4)], axis=1)
    pre_act = matmul(normed_low, whole)
    phi = 0.5 * (1.0 + lax.erf(pre_act * 0.7071067811865476))
    hidden = pre_act * phi
    w2_float = w2[...].astype(f32).reshape(1, pre_act.shape[1])
    logits = jnp.sum(hidden * w2_float, axis=1, keepdims=True)
    square = lax.broadcasted_iota(jnp.int32, (16, 16), 0) == lax.broadcasted_iota(jnp.int32, (16, 16), 1)
    target = jnp.sum(
        jnp.where(square, jnp.broadcast_to(lab[...], (16, 16)).astype(f32), 0.0), axis=1, keepdims=True
    )
    soft = jnp.exp(-jnp.abs(logits))
    loss_part = jnp.sum(jnp.maximum(logits, 0.0) + jnp.log1p(soft) - target * logits, axis=0, keepdims=True)
    logit_grad = jnp.where(logits >= 0.0, 1.0, soft) / (1.0 + soft) - target
    w2_part = jnp.sum(logit_grad * hidden, axis=0, keepdims=True)
    pre_grad = logit_grad * w2_float * gelu_slope(pre_act, phi)

    upper, lower = split(pre_grad)
    both = matmul(jnp.concatenate([upper, lower], axis=0), whole, NT)
    norm_grad = both[:16] + both[16:]
    pool_grad = (norm_grad - normed * (jnp.sum(norm_grad * normed, axis=1, keepdims=True) / width)) / root_mean

    product = pooled * pool_grad
    weight = jnp.exp(top - slide_top) / slide_total
    lane_pair = lax.broadcasted_iota(jnp.int32, (16, 384), 1)
    for q in range(4):
        grads = pool_grad[:, 384 * q : 384 * q + 384]
        terms = product[:, 384 * q : 384 * q + 384]
        pair = jnp.concatenate(
            [jnp.where(lane_pair < 192, grads, 0.0), jnp.where(lane_pair >= 192, grads, 0.0)], axis=0
        )
        upper, lower = split(pair)
        both = matmul(jnp.concatenate([upper, lower], axis=0), tiles[:, 384 * q : 384 * q + 384], NT)
        both = both[:32] + both[32:]
        for half in range(2):
            k = 2 * q + half
            side = lane_pair < 192 if half == 0 else lane_pair >= 192
            inner = jnp.sum(jnp.where(side, terms, 0.0), axis=1, keepdims=True)
            change = expo[16 * k : 16 * k + 16, :] * ((both[16 * half : 16 * half + 16] - inner) * weight[:, k : k + 1])
            delta[k : k + 1, :] = jnp.sum(change, axis=0, keepdims=True)

    upper, lower = split(delta[...])
    change = jnp.concatenate([upper, lower], axis=0)

    def score_part(half):
        both = matmul(change, gated[:, pl.ds(pl.multiple_of(256 * half, 256), 256)])
        return both[:8] + both[8:]

    gs_out[...] = score_part(1 - c)
    gs_swap = remote(gs_out, gs_in, gs_sem.at[0], gs_sem.at[1], tile=other_t)
    gs_swap.start()
    part = score_part(c)
    gs_swap.wait()
    part = part + gs_in[...]

    gz[z] = jnp.concatenate([part[:, :128], part[:, 128:]], axis=0).astype(bf16)

    def gs_z(i):
        return remote(gz.at[z], gz.at[z], gz_sem.at[0], gz_sem.at[1], **z_peer(i))

    loop(15, lambda i: gs_z(i).start())
    sent.append(lambda: drain(gz.at[pl.ds(0, 15)], gz_sem.at[0]))

    wide[:, :width] = normed_low.astype(f32)
    wide[:, width:] = jnp.zeros((16, 128), f32)
    first = 48 * t
    window = wide[:, pl.ds(pl.multiple_of(first // 128 * 128, 128), 256)].astype(bf16)
    chosen = lax.broadcasted_iota(jnp.int32, (256, 128), 0) == (
        lax.broadcasted_iota(jnp.int32, (256, 128), 1) + first % 128
    )
    normed_own = matmul(window, jnp.where(chosen, 1.0, 0.0).astype(bf16))
    sub = lax.broadcasted_iota(jnp.int32, (16, 128), 0)
    extra = jnp.zeros((16, 128), f32)
    for j in range(5):
        piece = w2_part[:, 128 * j : 128 * j + 128] if j < 4 else jnp.broadcast_to(loss_part, (1, 128))
        upper = piece.astype(bf16).astype(f32)
        extra = jnp.where(sub == j, upper, extra)
        extra = jnp.where(sub == 8 + j, piece - upper, extra)
    msg[d] = jnp.concatenate([pre_grad, normed_own, extra], axis=1).astype(bf16)

    def message(i):
        return remote(msg.at[d], msg.at[d], msg_sem.at[0], msg_sem.at[1], **dp_peer(i))

    loop(15, lambda i: message(i).start())
    sent.append(lambda: drain(msg.at[pl.ds(0, 15)], msg_sem.at[0]))

    drain(gz.at[pl.ds(0, 15)], gz_sem.at[1])

    ga[place] = jnp.sum(gz[...].astype(f32), axis=0).astype(bf16)

    def gs_plane(i):
        return remote(ga.at[place], ga.at[place], ga_sem.at[0], ga_sem.at[1], **plane_peer(i))

    loop(31, lambda i: gs_plane(i).start())
    sent.append(lambda: drain(ga.at[pl.ds(0, 31)], ga_sem.at[0]))
    drain(msg.at[pl.ds(0, 15)], msg_sem.at[1])
    grads = msg[:, :, 0:512].reshape(256, 512)
    own = msg[:, :, 512:640].reshape(256, 128)
    gw1_ref[...] = matmul(own, grads, TN)[:48]
    sums = jnp.sum(msg[:, :, 640:768].astype(f32), axis=0)
    sums = sums[:8] + sums[8:]
    gw2_ref[...] = jnp.concatenate([sums[j : j + 1] for j in range(4)], axis=1)
    loss_ref[...] = sums[4:5, 0:1] * (1.0 / 256.0)

    drain(ga.at[pl.ds(0, 31)], ga_sem.at[1])
    parts = ga[...].astype(f32).reshape(16, 2, 16, 128)
    for half in range(2):
        sums = jnp.sum(parts[:, half], axis=0)
        gs_ref[:, 256 * half : 256 * half + 128] = sums[:8]
        gs_ref[:, 256 * half + 128 : 256 * half + 256] = sums[8:]

    finish()


def body(tiles, slide_of_tile, labels, attn_v, attn_u, score_w, head_w1, head_w2):
    rows, width = tiles.shape
    hid = attn_v.shape[1]
    vmem, hbm = pl.BlockSpec(memory_space=pltpu.VMEM), pl.BlockSpec(memory_space=pltpu.HBM)
    dma = pltpu.SemaphoreType.DMA
    shapes = tuple(jax.ShapeDtypeStruct(shape, f32) for shape in ((48, hid), (8, hid), (1, hid), (1, 1)))
    results = pl.pallas_call(
        kernel,
        out_shape=tuple(pltpu.VMEM(x.shape, f32) for x in shapes),
        in_specs=[hbm] * 8,
        out_specs=(vmem, vmem, vmem, vmem),
        scratch_shapes=[
            pltpu.VMEM((rows, width), bf16),
            pltpu.VMEM((1, rows), jnp.int32),
            pltpu.VMEM((1, 16), jnp.int32),
            pltpu.VMEM((width, hid), bf16),
            pltpu.VMEM((width, hid), bf16),
            pltpu.VMEM((8, hid), bf16),
            pltpu.VMEM((hid,), bf16),
            pltpu.VMEM((rows, hid), bf16),
            pltpu.VMEM((8, rows), f32),
            pltpu.VMEM((128, rows), f32),
            pltpu.VMEM((4, 4, 4, 2, 48, 128), bf16),
            pltpu.VMEM((8, rows), f32),
            pltpu.VMEM((128, 128), f32),
            pltpu.VMEM((128, 128), f32),
            pltpu.VMEM((128, 128), f32),
            pltpu.VMEM((128, 128), f32),
            pltpu.VMEM((128, 128), f32),
            pltpu.VMEM((128, 128), f32),
            pltpu.VMEM((16, width + 128), f32),
            pltpu.VMEM((16, 16, 768), bf16),
            pltpu.VMEM((8, 256), f32),
            pltpu.VMEM((8, 256), f32),
            pltpu.VMEM((16, 16, 128), bf16),
            pltpu.VMEM((32, 16, 128), bf16),
            dma((12,)), dma((6,)), dma((4,)), dma((2,)), dma((2,)), dma((2,)), dma((2,)), dma((2,)), dma((2,)),
        ],
        compiler_params=pltpu.CompilerParams(
            collective_id=0, has_side_effects=True, vmem_limit_bytes=60 * 1024 * 1024
        ),
    )(tiles, slide_of_tile, labels, attn_v, attn_u, score_w.T, head_w1, head_w2)
    grad_w1, grad_score, grad_w2, loss = results
    return grad_w1, grad_score.T, grad_w2.reshape(hid), loss.reshape(())


def solution(mesh):
    return jax.shard_map(
        body,
        mesh=mesh,
        in_specs=(
            P(("dp", "tile"), None),
            P("dp", "tile"),
            P("dp", None),
            P(),
            P(),
            P(),
            P("tile", None),
            P(),
        ),
        out_specs=(P("tile", None), P(), P(), P()),
        check_vma=False,
    )
```

```python
import functools

import jax
import jax.numpy as jnp
from jax import lax
from jax.experimental import pallas as pl
from jax.experimental.pallas import tpu as pltpu
from jax.sharding import PartitionSpec as P

f32, bf16 = jnp.float32, jnp.bfloat16
MESH = pl.DeviceIdType.MESH
LOW = -3.0e38
BLOCK = 256
NN = (((1,), (0,)), ((), ()))
NT = (((1,), (1,)), ((), ()))
TN = (((0,), (0,)), ((), ()))


def matmul(a, b, dims=NN):
    return lax.dot_general(a, b, dims, preferred_element_type=f32)


def split(values):
    upper = values.astype(bf16)
    return upper, (values - upper.astype(f32)).astype(bf16)


def gelu_slope(values, phi):
    return phi + values * jnp.exp(-0.5 * values * values) * 0.3989422804014327


def remote(src, dst, send, recv, **where):
    return pltpu.make_async_remote_copy(
        src_ref=src, dst_ref=dst, send_sem=send, recv_sem=recv,
        device_id=where, device_id_type=MESH,
    )


def drain(ref, sem):
    pltpu.make_async_copy(ref, ref, sem).wait()


def kernel(
    tiles_hbm, seg_hbm, lab_hbm, v_hbm, u_hbm, sw_hbm, w1_hbm, w2_hbm,
    gw1_ref, gs_ref, gw2_ref, loss_ref,
    tiles, seg, lab, wv, wu, sw, w2,
    gated, scores, expo, w1, delta,
    swap_out, swap_in, red_out, red_in, own_half, other_half,
    wide, msg, gs_out, gs_in, gz, ga,
    load_sem, w1_sem, half_sem, red_sem, all_sem, msg_sem, gs_sem, gz_sem, ga_sem,
):
    d, t = lax.axis_index("dp"), lax.axis_index("tile")
    z, c = t // 2, t % 2
    other_t = 2 * z + 1 - c
    dx, dy = d // 4, d % 4
    rows = tiles.shape[0]
    sent = []

    def finish():
        for wait in sent:
            wait()

    def loop(count, step):
        def go(i, carry):
            step(i)
            return carry

        lax.fori_loop(0, count, go, 0)

    barrier = pltpu.get_barrier_semaphore()

    place = 2 * d + c

    def turn(i):
        return 2 + 3 * i + 3 * (i * (i - 1) // 2)

    def dp_peer(i):
        return {"dp": (dx + turn(i // 4)) % 4 * 4 + (dy + turn(i % 4)) % 4}

    def plane_peer(i):
        return {**dp_peer(i // 2), "tile": 2 * z + (c + 1 + i) % 2}

    def z_place(i):
        return (z + 8 + (1 - 2 * (i % 2)) * ((i + 1) // 2)) % 16

    def z_peer(i):
        return {"tile": 2 * z_place(i) + c}

    def greet(who):
        pl.semaphore_signal(barrier, inc=1, device_id=who, device_id_type=MESH)

    loop(15, lambda i: greet(z_peer(i)))

    loads = [
        pltpu.make_async_copy(v_hbm, wv, load_sem.at[0]),
        pltpu.make_async_copy(u_hbm, wu, load_sem.at[1]),
    ]
    for b in range(rows // BLOCK):
        part = pl.ds(b * BLOCK, BLOCK)
        loads.append(pltpu.make_async_copy(tiles_hbm.at[part], tiles.at[part], load_sem.at[2 + b]))
    small = [
        pltpu.make_async_copy(sw_hbm, sw, load_sem.at[8]),
        pltpu.make_async_copy(seg_hbm, seg, load_sem.at[9]),
        pltpu.make_async_copy(lab_hbm, lab, load_sem.at[10]),
        pltpu.make_async_copy(w2_hbm, w2, load_sem.at[11]),
    ]
    own_w1 = pltpu.make_async_copy(
        w1_hbm.at[:, pl.ds(pl.multiple_of(dx * 128, 128), 128)],
        w1.at[dx, z // 4, z % 4, c], load_sem.at[7],
    )
    for load in [loads[2], *loads[:2], small[0], *loads[3:], *small[1:]]:
        load.start()

    loop(31, lambda i: greet(plane_peer(i)))


    def w1_first(i):
        return remote(
            w1_hbm.at[:, pl.ds(pl.multiple_of(dx * 128, 128), 128)],
            w1.at[dx, z // 4, z % 4, c], w1_sem.at[0], w1_sem.at[1], **z_peer(i),
        )

    def w1_second(half, i):
        part = w1.at[dx, pl.ds(2 * half, 2), dy, c]
        return remote(part, part, w1_sem.at[2 + half], w1_sem.at[4 + half], **dp_peer(i))

    def w1_third(half):
        part = w1.at[:, pl.ds(2 * half, 2), :, c]
        return remote(part, part, w1_sem.at[6 + half], w1_sem.at[8 + half], tile=other_t)

    def w1_start():
        @pl.when(z % 4 == dy)
        def _():
            own_w1.start()
            loop(15, lambda i: w1_first(i).start())

        def wait_first():
            @pl.when(z % 4 == dy)
            def _():
                loop(15, lambda i: w1_first(i).wait_send())

        sent.append(wait_first)

    def w1_middle():
        @pl.when(z % 4 == dy)
        def _():
            own_w1.wait()
            drain(w1.at[0, pl.ds(0, 3), 0, 0], w1_sem.at[1])

        @pl.when(z % 4 != dy)
        def _():
            drain(w1.at[0, :, 0, 0], w1_sem.at[1])

        loop(15, lambda i: w1_second(0, i).start())
        loop(15, lambda i: w1_second(1, i).start())
        sent.append(lambda: drain(tiles_hbm.at[pl.ds(0, 120)], w1_sem.at[2]))
        sent.append(lambda: drain(tiles_hbm.at[pl.ds(0, 120)], w1_sem.at[3]))

    def w1_last():
        for half in range(2):
            drain(tiles_hbm.at[pl.ds(0, 120)], w1_sem.at[4 + half])
            w1_third(half).start()

    def w1_end():
        w1_third(0).wait()
        w1_third(1).wait()

    def scorer(b):
        part = pl.ds(b * BLOCK, BLOCK)
        x = tiles[part, :]
        if b == 0:
            loads[0].wait()
        tanh_part = jnp.tanh(matmul(x, wv[...]))
        if b == 0:
            loads[1].wait()
            small[0].wait()
        gate_part = 0.5 + 0.5 * jnp.tanh(0.5 * matmul(x, wu[...]))
        low = (tanh_part * gate_part).astype(bf16)
        gated[part, :] = low
        scores[:, part] = matmul(sw[...], low, NT)

    for b in range(rows // BLOCK):
        if b == 2:
            pl.semaphore_wait(barrier, 46)
            w1_start()
        loads[2 + b].wait()
        scorer(b)
    for load in small[1:]:
        load.wait()

    member = lax.broadcasted_iota(jnp.int32, (16, rows), 0) == seg[...]
    lane = lax.broadcasted_iota(jnp.int32, (16, 128), 1)
    top = jnp.full((16, 128), LOW, f32)
    total = jnp.zeros((16, 128), f32)
    for k in range(8):
        score = jnp.broadcast_to(scores[k : k + 1, :], (16, rows))
        peak = jnp.max(jnp.where(member, score, LOW), axis=1, keepdims=True)
        term = jnp.where(member, jnp.exp(score - peak), 0.0)
        expo[16 * k : 16 * k + 16, :] = term
        top = jnp.where(lane == k, peak, top)
        total = jnp.where(lane == k, jnp.sum(term, axis=1, keepdims=True), total)

    def pool(half):
        blocks = []
        for i in range(2):
            upper, lower = split(expo[pl.ds(pl.multiple_of(64 * half + 32 * i, 32), 32), :])
            part = tiles[:, pl.ds(pl.multiple_of(768 * half + 384 * i, 128), 384)]
            both = matmul(jnp.concatenate([upper, lower], axis=0), part)
            both = both[:32] + both[32:]
            first, second = both[:16], both[16:]
            blocks += [
                first[:, :128],
                jnp.where(lane < 64, first[:, 128:256], second[:, 128:256]),
                second[:, 256:],
            ]
        return blocks

    def pick(a, b):
        return jnp.where(c == 0, a, b)

    def strided(j):
        return pl.ds(j, 16, stride=8)

    for j, block in enumerate(pool(1 - c)):
        swap_out[strided(j), :] = block
    swap_out[strided(6), :] = total
    swap_out[strided(7), :] = top
    swap = remote(swap_out, swap_in, half_sem.at[0], half_sem.at[1], tile=other_t)
    swap.start()
    mine = pool(c)
    swap.wait()

    low_lane = lane < 64

    def spread(table):
        heads = [pick(table[:, k : k + 1], table[:, 4 + k : 5 + k]) for k in range(4)]
        n = table.shape[0]
        heads = [jnp.broadcast_to(h, (n, 128)) for h in heads]
        low = low_lane[:n]
        return [
            heads[0], jnp.where(low, heads[0], heads[1]), heads[1],
            heads[2], jnp.where(low, heads[2], heads[3]), heads[3],
        ]

    top_other = swap_in[strided(7), :]
    pair_top = jnp.maximum(top, top_other)
    scale, scale_other = jnp.exp(top - pair_top), jnp.exp(top_other - pair_top)
    wide_own, wide_other = spread(scale), spread(scale_other)
    for j in range(6):
        red_out[strided(j), :] = mine[j] * wide_own[j] + swap_in[strided(j), :] * wide_other[j]
    red_out[strided(6), :] = total * scale + swap_in[strided(6), :] * scale_other
    red_out[strided(7), :] = pair_top

    def eight(i):
        return pl.ds(pl.multiple_of(8 * i, 8), 8)

    def reduce_copy(i):
        return remote(red_out.at[eight(z_place(i))], red_in.at[eight(z)], red_sem.at[0], red_sem.at[1], **z_peer(i))

    loop(15, lambda i: reduce_copy(i).start())
    sent.append(lambda: drain(red_in.at[pl.ds(0, 120)], red_sem.at[0]))
    red_in[eight(z), :] = red_out[eight(z), :]

    w1_middle()

    drain(red_in.at[pl.ds(0, 120)], red_sem.at[1])
    tops = red_in[strided(7), :]
    slide_top = jnp.max(tops, axis=0, keepdims=True)
    scale = jnp.exp(tops - slide_top)
    slide_total = jnp.sum(red_in[strided(6), :] * scale, axis=0, keepdims=True)
    wide_scale, wide_total = spread(scale), spread(slide_total)
    tile_rows = [
        jnp.sum(red_in[strided(j), :] * wide_scale[j], axis=0, keepdims=True) / wide_total[j]
        for j in range(6)
    ]
    own_half[eight(z), :] = jnp.concatenate(tile_rows + [slide_total, slide_top], axis=0)

    def gather_copy(i):
        return remote(own_half.at[eight(z)], own_half.at[eight(z)], all_sem.at[0], all_sem.at[1], **z_peer(i))

    loop(15, lambda i: gather_copy(i).start())
    sent.append(lambda: drain(own_half.at[pl.ds(0, 120)], all_sem.at[0]))
    w1_last()
    drain(own_half.at[pl.ds(0, 120)], all_sem.at[1])
    relay = remote(own_half, other_half, half_sem.at[2], half_sem.at[3], tile=other_t)
    relay.start()
    w1_end()
    relay.wait()

    left, right = [], []
    for j in range(6):
        a, b = own_half[strided(j), :], other_half[strided(j), :]
        left.append(pick(a, b))
        right.append(pick(b, a))
    pooled = jnp.concatenate(left + right, axis=1)
    slide_total, slide_top = own_half[strided(6), :], own_half[strided(7), :]
    width = pooled.shape[1]
    root_mean = jnp.sqrt(jnp.sum(pooled * pooled, axis=1, keepdims=True) / width + 1e-5)
    normed = pooled / root_mean
    normed_low = normed.astype(bf16)
    whole = jnp.concatenate([w1[x].reshape(width, 128) for x in range(4)], axis=1)
    pre_act = matmul(normed_low, whole)
    phi = 0.5 * (1.0 + lax.erf(pre_act * 0.7071067811865476))
    hidden = pre_act * phi
    w2_float = w2[...].astype(f32).reshape(1, pre_act.shape[1])
    logits = jnp.sum(hidden * w2_float, axis=1, keepdims=True)
    square = lax.broadcasted_iota(jnp.int32, (16, 16), 0) == lax.broadcasted_iota(jnp.int32, (16, 16), 1)
    target = jnp.sum(
        jnp.where(square, jnp.broadcast_to(lab[...], (16, 16)).astype(f32), 0.0), axis=1, keepdims=True
    )
    soft = jnp.exp(-jnp.abs(logits))
    loss_part = jnp.sum(jnp.maximum(logits, 0.0) + jnp.log1p(soft) - target * logits, axis=0, keepdims=True)
    logit_grad = jnp.where(logits >= 0.0, 1.0, soft) / (1.0 + soft) - target
    w2_part = jnp.sum(logit_grad * hidden, axis=0, keepdims=True)
    pre_grad = logit_grad * w2_float * gelu_slope(pre_act, phi)

    upper, lower = split(pre_grad)
    both = matmul(jnp.concatenate([upper, lower], axis=0), whole, NT)
    norm_grad = both[:16] + both[16:]
    pool_grad = (norm_grad - normed * (jnp.sum(norm_grad * normed, axis=1, keepdims=True) / width)) / root_mean

    product = pooled * pool_grad
    weight = jnp.exp(top - slide_top) / slide_total
    lane_pair = lax.broadcasted_iota(jnp.int32, (16, 384), 1)
    for q in range(4):
        grads = pool_grad[:, 384 * q : 384 * q + 384]
        terms = product[:, 384 * q : 384 * q + 384]
        pair = jnp.concatenate(
            [jnp.where(lane_pair < 192, grads, 0.0), jnp.where(lane_pair >= 192, grads, 0.0)], axis=0
        )
        upper, lower = split(pair)
        both = matmul(jnp.concatenate([upper, lower], axis=0), tiles[:, 384 * q : 384 * q + 384], NT)
        both = both[:32] + both[32:]
        for half in range(2):
            k = 2 * q + half
            side = lane_pair < 192 if half == 0 else lane_pair >= 192
            inner = jnp.sum(jnp.where(side, terms, 0.0), axis=1, keepdims=True)
            change = expo[16 * k : 16 * k + 16, :] * ((both[16 * half : 16 * half + 16] - inner) * weight[:, k : k + 1])
            delta[k : k + 1, :] = jnp.sum(change, axis=0, keepdims=True)

    upper, lower = split(delta[...])
    change = jnp.concatenate([upper, lower], axis=0)

    def score_part(half):
        both = matmul(change, gated[:, pl.ds(pl.multiple_of(256 * half, 256), 256)])
        return both[:8] + both[8:]

    gs_out[...] = score_part(1 - c)
    gs_swap = remote(gs_out, gs_in, gs_sem.at[0], gs_sem.at[1], tile=other_t)
    gs_swap.start()
    part = score_part(c)
    gs_swap.wait()
    part = part + gs_in[...]

    gz[z] = jnp.concatenate([part[:, :128], part[:, 128:]], axis=0).astype(bf16)

    def gs_z(i):
        return remote(gz.at[z], gz.at[z], gz_sem.at[0], gz_sem.at[1], **z_peer(i))

    loop(15, lambda i: gs_z(i).start())
    sent.append(lambda: drain(gz.at[pl.ds(0, 15)], gz_sem.at[0]))

    wide[:, :width] = normed_low.astype(f32)
    wide[:, width:] = jnp.zeros((16, 128), f32)
    first = 48 * t
    window = wide[:, pl.ds(pl.multiple_of(first // 128 * 128, 128), 256)].astype(bf16)
    chosen = lax.broadcasted_iota(jnp.int32, (256, 128), 0) == (
        lax.broadcasted_iota(jnp.int32, (256, 128), 1) + first % 128
    )
    normed_own = matmul(window, jnp.where(chosen, 1.0, 0.0).astype(bf16))
    sub = lax.broadcasted_iota(jnp.int32, (16, 128), 0)
    extra = jnp.zeros((16, 128), f32)
    for j in range(5):
        piece = w2_part[:, 128 * j : 128 * j + 128] if j < 4 else jnp.broadcast_to(loss_part, (1, 128))
        upper = piece.astype(bf16).astype(f32)
        extra = jnp.where(sub == j, upper, extra)
        extra = jnp.where(sub == 8 + j, piece - upper, extra)
    msg[d] = jnp.concatenate([pre_grad, normed_own, extra], axis=1).astype(bf16)

    def message(i):
        return remote(msg.at[d], msg.at[d], msg_sem.at[0], msg_sem.at[1], **dp_peer(i))

    loop(15, lambda i: message(i).start())
    sent.append(lambda: drain(msg.at[pl.ds(0, 15)], msg_sem.at[0]))

    drain(gz.at[pl.ds(0, 15)], gz_sem.at[1])

    ga[place] = jnp.sum(gz[...].astype(f32), axis=0).astype(bf16)

    def gs_plane(i):
        return remote(ga.at[place], ga.at[place], ga_sem.at[0], ga_sem.at[1], **plane_peer(i))

    loop(31, lambda i: gs_plane(i).start())
    sent.append(lambda: drain(ga.at[pl.ds(0, 31)], ga_sem.at[0]))
    drain(msg.at[pl.ds(0, 15)], msg_sem.at[1])
    grads = msg[:, :, 0:512].reshape(256, 512)
    own = msg[:, :, 512:640].reshape(256, 128)
    gw1_ref[...] = matmul(own, grads, TN)[:48]
    sums = jnp.sum(msg[:, :, 640:768].astype(f32), axis=0)
    sums = sums[:8] + sums[8:]
    gw2_ref[...] = jnp.concatenate([sums[j : j + 1] for j in range(4)], axis=1)
    loss_ref[...] = sums[4:5, 0:1] * (1.0 / 256.0)

    drain(ga.at[pl.ds(0, 31)], ga_sem.at[1])
    parts = ga[...].astype(f32).reshape(16, 2, 16, 128)
    for half in range(2):
        sums = jnp.sum(parts[:, half], axis=0)
        gs_ref[:, 256 * half : 256 * half + 128] = sums[:8]
        gs_ref[:, 256 * half + 128 : 256 * half + 256] = sums[8:]

    finish()


def body(tiles, slide_of_tile, labels, attn_v, attn_u, score_w, head_w1, head_w2):
    rows, width = tiles.shape
    hid = attn_v.shape[1]
    vmem, hbm = pl.BlockSpec(memory_space=pltpu.VMEM), pl.BlockSpec(memory_space=pltpu.HBM)
    dma = pltpu.SemaphoreType.DMA
    shapes = tuple(jax.ShapeDtypeStruct(shape, f32) for shape in ((48, hid), (8, hid), (1, hid), (1, 1)))
    results = pl.pallas_call(
        kernel,
        out_shape=tuple(pltpu.VMEM(x.shape, f32) for x in shapes),
        in_specs=[hbm] * 8,
        out_specs=(vmem, vmem, vmem, vmem),
        scratch_shapes=[
            pltpu.VMEM((rows, width), bf16),
            pltpu.VMEM((1, rows), jnp.int32),
            pltpu.VMEM((1, 16), jnp.int32),
            pltpu.VMEM((width, hid), bf16),
            pltpu.VMEM((width, hid), bf16),
            pltpu.VMEM((8, hid), bf16),
            pltpu.VMEM((hid,), bf16),
            pltpu.VMEM((rows, hid), bf16),
            pltpu.VMEM((8, rows), f32),
            pltpu.VMEM((128, rows), f32),
            pltpu.VMEM((4, 4, 4, 2, 48, 128), bf16),
            pltpu.VMEM((8, rows), f32),
            pltpu.VMEM((128, 128), f32),
            pltpu.VMEM((128, 128), f32),
            pltpu.VMEM((128, 128), f32),
            pltpu.VMEM((128, 128), f32),
            pltpu.VMEM((128, 128), f32),
            pltpu.VMEM((128, 128), f32),
            pltpu.VMEM((16, width + 128), f32),
            pltpu.VMEM((16, 16, 768), bf16),
            pltpu.VMEM((8, 256), f32),
            pltpu.VMEM((8, 256), f32),
            pltpu.VMEM((16, 16, 128), bf16),
            pltpu.VMEM((32, 16, 128), bf16),
            dma((12,)), dma((10,)), dma((4,)), dma((2,)), dma((2,)), dma((2,)), dma((2,)), dma((2,)), dma((2,)),
        ],
        compiler_params=pltpu.CompilerParams(
            collective_id=0, has_side_effects=True, vmem_limit_bytes=60 * 1024 * 1024
        ),
    )(tiles, slide_of_tile, labels, attn_v, attn_u, score_w.T, head_w1, head_w2)
    grad_w1, grad_score, grad_w2, loss = results
    return grad_w1, grad_score.T, grad_w2.reshape(hid), loss.reshape(())


def solution(mesh):
    return jax.shard_map(
        body,
        mesh=mesh,
        in_specs=(
            P(("dp", "tile"), None),
            P("dp", "tile"),
            P("dp", None),
            P(),
            P(),
            P(),
            P("tile", None),
            P(),
        ),
        out_specs=(P("tile", None), P(), P(), P()),
        check_vma=False,
    )
```
